32 devices in a mesh: chan: 4 (over y, x), ctx: 8 (over z, core).
Axes of the slice: x: 2, y: 2, z: 4, core: 2. Of those that a mesh axis runs over, the one named last changes fastest.
Arguments:
- inputs: bfloat16 [1024, 4096], P('ctx', 'chan'), may hold values from -0.1875 to 0.1875
- filter_taps: bfloat16 [1024, 4096], P('ctx', 'chan'), may hold values from -0.1875 to 0.1875
- out_grad: bfloat16 [1024, 4096], P('ctx', 'chan')
- skip_gain: float32 [4096], P('chan'), may hold values from 0.5 to 2
Outputs:
- input_grad: float32 [1024, 4096], P('ctx', 'chan')
- filter_grad: float32 [1024, 4096], P('ctx', 'chan')
- skip_grad: float32 [4096], P('chan')
The draws below stay inside these ranges and needn't reach their ends.
All inputs are finite; a program needn't handle non-finite values.
Results may differ from the reference program's by a relative error of at most 0.0003.
Values may be sent and summed in bfloat16 or wider, within the bound.
No kernel may reach another device: no remote copies, remote signals or barrier semaphores. Data moves between devices by JAX's collectives and lax.ppermute only.
A program may use at most 64 MiB of HBM per device.

```python
import math
import jax
import jax.numpy as jnp
from jax import lax

CHANNELS = 4096
SEQ = 1024


def draw_out_grad(key, part):
    key = jax.random.fold_in(key, 7)
    subkeys = jax.random.split(key, 3)
    row_scale = jnp.exp(jax.random.uniform(subkeys[0], (SEQ, 1), jnp.float32, -1.15, 1.15))
    col_scale = jnp.exp(jax.random.uniform(subkeys[1], (1, CHANNELS), jnp.float32, -1.15, 1.15))
    values = jax.random.normal(subkeys[2], (SEQ, CHANNELS), jnp.float32)
    return (row_scale * col_scale * values).astype(jnp.bfloat16)


def steps_of(key, extent, cuts, smallest, high):
    def one(position, blocks):
        draws = jax.random.uniform(jax.random.fold_in(jax.random.fold_in(key, 6), position), (blocks,), jnp.float32, smallest / len(cuts), high / len(cuts))
        return jnp.repeat(jnp.exp(draws), extent[position] // blocks).reshape((-1,) + (1,) * (len(extent) - position - 1))

    level = one(*cuts[0])
    for cut in cuts[1:]:
        level = level * one(*cut)
    return level


def centred(own_key, extent, scale, most, cuts=(), dtype=jnp.bfloat16):
    entries = scale * jax.random.normal(own_key, extent, jnp.float32)
    if cuts:
        entries = entries * steps_of(own_key, extent, cuts, -0.22, 0.18)
    return jnp.clip(entries, -most, most).astype(dtype)


def setup_inputs(seed: int = 0) -> dict:
    key_list = jax.random.split(jax.random.key(seed), 5)
    return {
        "inputs": centred(key_list[0], (SEQ, CHANNELS), SEQ ** -0.5, 0.1875, ((0, 8), (1, 4))),
        "filter_taps": centred(key_list[1], (SEQ, CHANNELS), SEQ ** -0.5, 0.1875, ((0, 8), (1, 4))),
        "out_grad": draw_out_grad(jax.random.fold_in(key_list[4], 71), 0),
        "skip_gain": jnp.clip(0.5 + 1.5 * jax.random.uniform(key_list[3], (CHANNELS,), jnp.float32) ** steps_of(key_list[3], (CHANNELS,), ((0, 4),), -0.2, 0.2), 0.5, 2.0),
    }


def correlate_block(grad_rows, other_rows):
    period = 2 * grad_rows.shape[0]
    product = jnp.fft.rfft(grad_rows, n=period, axis=0) * jnp.conj(jnp.fft.rfft(other_rows, n=period, axis=0))
    return jnp.fft.irfft(product, n=period, axis=0)[:grad_rows.shape[0]]

def reference(inputs, filter_taps, out_grad, skip_gain):
    grad_rows = out_grad.astype(jnp.float32)
    input_rows = inputs.astype(jnp.float32)
    filter_rows = filter_taps.astype(jnp.float32)
    block_width = math.gcd(CHANNELS, 256)
    block_count = CHANNELS // block_width

    def to_blocks(array):
        return array.reshape(SEQ, block_count, block_width).transpose(1, 0, 2)

    def from_blocks(array):
        return array.transpose(1, 0, 2).reshape(SEQ, CHANNELS)

    def per_block(blocks):
        grad_part, input_part, filter_part = blocks
        return (correlate_block(grad_part, filter_part), correlate_block(grad_part, input_part))
    conv_in, raw_grad = lax.map(per_block, (to_blocks(grad_rows), to_blocks(input_rows), to_blocks(filter_rows)))
    input_grad = from_blocks(conv_in) + skip_gain[None, :] * grad_rows
    raw_grad = from_blocks(raw_grad)
    norm_square = jnp.sum(raw_grad * raw_grad)
    clip_limit = 0.25 * math.sqrt(SEQ * CHANNELS)
    factor = jnp.minimum(1.0, clip_limit / jnp.sqrt(norm_square + 1e-06))
    filter_grad = raw_grad * factor
    skip_grad = lax.optimization_barrier(jnp.sum(grad_rows * input_rows, axis=0))
    return (input_grad, filter_grad, skip_grad)
```

```python
import functools
import math

import jax
import jax.numpy as jnp
import numpy as np
from jax import lax
from jax.experimental import pallas as pl
from jax.experimental.pallas import tpu as pltpu
from jax.sharding import PartitionSpec as P

epsilon = 1e-06
octaves = 246
low_power = 120
top_code = 128 * octaves - 1
tail_rows = 16
vmem_bytes = 48 * 1024 * 1024


def tables(length):
    odd = 2 * np.arange(length) + 1
    phase = odd[:, None] * np.arange(length)[None, :] % (4 * length)
    angles = np.pi * phase / (2 * length)
    forward = np.concatenate([np.cos(angles), -np.sin(angles)], axis=0)
    high = forward.astype(np.float32).astype(jnp.bfloat16)
    low = (forward - high.astype(np.float64)).astype(np.float32).astype(jnp.bfloat16)
    both = np.concatenate([high, low], axis=1)
    scale = np.float32(1.0 / length)
    back_high = (high.astype(np.float32).T * scale).astype(jnp.bfloat16)
    back_low = (low.astype(np.float32).T * scale).astype(jnp.bfloat16)
    return jnp.asarray(both), jnp.asarray(back_high), jnp.asarray(back_low)


def three_parts(value):
    high = value.astype(jnp.bfloat16).astype(jnp.float32)
    rest = value - high
    middle = rest.astype(jnp.bfloat16).astype(jnp.float32)
    return high, middle, rest - middle


def encode(values):
    peak = jnp.max(jnp.abs(values), axis=0, keepdims=True) * (1.0 + 2.0**-7)
    scale = jnp.maximum(peak.astype(jnp.bfloat16).astype(jnp.float32), 2.0**-110)
    units = values * (top_code / scale)
    code = jnp.minimum(jnp.floor(jnp.abs(units) + 0.5), float(top_code))
    octave = jnp.floor(code * (1.0 / 128))
    mantissa = 1.0 + (code - 128.0 * octave) * (1.0 / 128)
    carrier = mantissa * jnp.exp2(octave - float(low_power))
    return jnp.where(units < 0, -carrier, carrier).astype(jnp.bfloat16), scale


def decode(codes, scale):
    carrier = codes.astype(jnp.float32)
    size = jnp.abs(carrier)
    power = jnp.floor(jnp.log2(size) + 0.001)
    mantissa = jnp.floor(size * jnp.exp2(-power) * 128.0 + 0.5)
    units = (power + float(low_power - 1)) * 128.0 + mantissa
    return jnp.where(carrier < 0, -units, units) * (scale * (1.0 / top_code))


def tail_tile(rows, width):
    row_ids = lax.broadcasted_iota(jnp.int32, (tail_rows, width), 0)
    tile = jnp.zeros((tail_rows, width), jnp.float32)
    for i, row in enumerate(rows):
        tile = jnp.where(row_ids == i, jnp.broadcast_to(row, (tail_rows, width)), tile)
    return tile.astype(jnp.bfloat16)


def correlate_rows(pairs, others, size):
    results = []
    for p in range(size):
        real = imag = None
        for q in range(p, size):
            (gr, gi), (fr, fi) = pairs[q], others[q - p]
            real_term = gr * fr + gi * fi
            imag_term = gi * fr - gr * fi
            real = real_term if real is None else real + real_term
            imag = imag_term if imag is None else imag + imag_term
        results.append((real, imag))
    return results


def send_results(position, size, acc, back_high, back_low, emit):
    width = acc.shape[2]
    for k in range(0, size, 2):
        spec = jnp.concatenate([acc[position ^ k], acc[position ^ (k + 1)]], axis=1)
        high = spec.astype(jnp.bfloat16)
        low = (spec - high.astype(jnp.float32)).astype(jnp.bfloat16)
        dot = functools.partial(jnp.dot, preferred_element_type=jnp.float32)
        block = dot(back_high[...], high) + dot(back_high[...], low) + dot(back_low[...], high)
        emit(k, block[:, :width])
        emit(k + 1, block[:, width:])


def first_kernel(size, length, *refs):
    arrived = refs[:size]
    both, back_high, back_low = refs[size : size + 3]
    out = refs[size + 3 : 2 * size + 3]
    pair_spec, squares, spec, acc = refs[2 * size + 3 :]
    width = spec.shape[2] // 2
    position = lax.axis_index("ctx")

    skip = jnp.zeros((1, width), jnp.float32)
    for k in range(size):
        grad, other = arrived[k][:length], arrived[k][length:]
        skip += jnp.sum(grad.astype(jnp.float32) * other.astype(jnp.float32), axis=0, keepdims=True)
        lanes = jnp.concatenate([grad, other], axis=1)
        spec[position ^ k] = jnp.dot(
            both[...], jnp.concatenate([lanes, lanes], axis=0), preferred_element_type=jnp.float32
        )

    flip = jnp.where(lax.broadcasted_iota(jnp.int32, (8, width), 0) % 2 == 0, 1.0, -1.0)

    def rows(r, carry):
        real_rows = pl.ds(pl.multiple_of(r * 8, 8), 8)
        imag_rows = pl.ds(pl.multiple_of(length + r * 8, 8), 8)
        grad = [(spec[q, real_rows, :width], spec[q, imag_rows, :width]) for q in range(size)]
        pairs = []
        for q in range(size):
            if q + 1 < size:
                real = grad[q][0] + flip * grad[q + 1][1]
                imag = grad[q][1] - flip * grad[q + 1][0]
            else:
                real, imag = grad[q]
            pair_spec[q, real_rows, :] = real
            pair_spec[q, imag_rows, :] = imag
            pairs.append((real, imag))
        others = [(spec[q, real_rows, width:], spec[q, imag_rows, width:]) for q in range(size)]
        for p, (real, imag) in enumerate(correlate_rows(pairs, others, size)):
            acc[p, real_rows, :] = real
            acc[p, imag_rows, :] = imag
        return carry

    lax.fori_loop(0, length // 8, rows, 0)
    skip_parts = three_parts(skip)
    squares[...] = jnp.zeros_like(squares)

    def emit(k, block):
        squares[...] += jnp.sum((block * block).reshape(length // 8, 8, width), axis=0)
        codes, scale = encode(block)
        out[k][:length] = codes
        out[k][length:] = tail_tile((scale,) + skip_parts, width)

    send_results(position, size, acc, back_high, back_low, emit)


def second_kernel(size, length, sums, *refs):
    arrived = refs[:size]
    both, back_high, back_low, pair_spec = refs[size : size + 4]
    partial_squares = refs[size + 4 : size + 4 + sums]
    out = refs[size + 4 + sums : 2 * size + 4 + sums]
    spec, acc = refs[2 * size + 4 + sums :]
    width = spec.shape[2]
    position = lax.axis_index("ctx")

    for k in range(0, size, 2):
        lanes = jnp.concatenate([arrived[k][...], arrived[k + 1][...]], axis=1)
        both_specs = jnp.dot(
            both[...], jnp.concatenate([lanes, lanes], axis=0), preferred_element_type=jnp.float32
        )
        spec[position ^ k] = both_specs[:, :width]
        spec[position ^ (k + 1)] = both_specs[:, width:]

    def rows(r, carry):
        real_rows = pl.ds(pl.multiple_of(r * 8, 8), 8)
        imag_rows = pl.ds(pl.multiple_of(length + r * 8, 8), 8)
        pairs = [(pair_spec[q, real_rows, :], pair_spec[q, imag_rows, :]) for q in range(size)]
        others = [(spec[q, real_rows, :], spec[q, imag_rows, :]) for q in range(size)]
        for p, (real, imag) in enumerate(correlate_rows(pairs, others, size)):
            acc[p, real_rows, :] = real
            acc[p, imag_rows, :] = imag
        return carry

    lax.fori_loop(0, length // 8, rows, 0)
    squares = partial_squares[0][...]
    for other in partial_squares[1:]:
        squares += other[...]
    total = jnp.sum(jnp.sum(squares, axis=0, keepdims=True), axis=1, keepdims=True)
    total_parts = three_parts(jnp.broadcast_to(total, (1, width)))

    def emit(k, block):
        codes, scale = encode(block)
        out[k][:length] = codes
        out[k][length:] = tail_tile((scale,) + total_parts, width)

    send_results(position, size, acc, back_high, back_low, emit)


def last_kernel(size, length, part, clip_limit, *refs):
    filter_codes, input_codes = refs[:size], refs[size : 2 * size]
    grad, gain, input_grad, filter_grad, skip_grad = refs[2 * size :]
    position = lax.axis_index("ctx")
    total = jnp.zeros((1, part), jnp.float32)
    for k in range(size):
        tail = input_codes[k][length:].astype(jnp.float32)
        total += tail[1:2] + tail[2:3] + tail[3:4]
    factor = jnp.minimum(1.0, clip_limit / jnp.sqrt(total + epsilon))
    for k in range(size):
        columns = pl.ds(pl.multiple_of((position ^ k) * part, part), part)
        tail = filter_codes[k][length:].astype(jnp.float32)
        filter_grad[:, columns] = decode(filter_codes[k][:length], tail[0:1]) * factor
        skip_grad[:, columns] = tail[1:2] + tail[2:3] + tail[3:4]
        tail = input_codes[k][length:].astype(jnp.float32)
        input_grad[:, columns] = (
            decode(input_codes[k][:length], tail[0:1])
            + gain[:, columns] * grad[:, columns].astype(jnp.float32)
        )


def run(kernel, name, out_shape, scratch=()):
    return pl.pallas_call(
        kernel,
        out_shape=out_shape,
        scratch_shapes=scratch,
        name=name,
        compiler_params=pltpu.CompilerParams(vmem_limit_bytes=vmem_bytes),
    )


def per_device(inputs, filter_taps, out_grad, skip_gain):
    length, chan_width = inputs.shape
    size = lax.axis_size("ctx")
    columns = lax.axis_size("chan")
    part = chan_width // size
    width = -(-part // 128) * 128
    position = lax.axis_index("ctx")
    both, back_high, back_low = tables(length)
    f32, bf16 = jnp.float32, jnp.bfloat16

    def columns_for(array, k):
        block = lax.dynamic_slice_in_dim(array, (position ^ k) * part, part, 1)
        return jnp.pad(block, ((0, 0), (0, width - part)))

    def exchange(blocks):
        return [
            blocks[k] if k == 0 else lax.ppermute(blocks[k], "ctx", [(i, i ^ k) for i in range(size)])
            for k in range(size)
        ]

    grad_input = exchange(
        [
            jnp.concatenate([columns_for(out_grad, k), columns_for(inputs, k)], axis=0)
            for k in range(size)
        ]
    )
    taps = exchange([columns_for(filter_taps, k) for k in range(size)])

    message = jax.ShapeDtypeStruct((length + tail_rows, width), bf16)
    *filter_codes, pair_spec, squares = run(
        functools.partial(first_kernel, size, length),
        "filter_gradient",
        [message] * size
        + [
            jax.ShapeDtypeStruct((size, 2 * length, width), f32),
            jax.ShapeDtypeStruct((8, width), f32),
        ],
        [
            pltpu.VMEM((size, 2 * length, 2 * width), f32),
            pltpu.VMEM((size, 2 * length, width), f32),
        ],
    )(*grad_input, both, back_high, back_low)
    filter_codes = exchange(filter_codes)
    all_squares = [
        squares if k == 0 else lax.ppermute(squares, "chan", [(i, i ^ k) for i in range(columns)])
        for k in range(columns)
    ]
    input_codes = run(
        functools.partial(second_kernel, size, length, columns),
        "input_gradient",
        [message] * size,
        [
            pltpu.VMEM((size, 2 * length, width), f32),
            pltpu.VMEM((size, 2 * length, width), f32),
        ],
    )(*taps, both, back_high, back_low, pair_spec, *all_squares)
    input_codes = exchange(input_codes)

    clip_limit = 0.25 * math.sqrt(length * size * chan_width * columns)
    whole = size * width
    grad_rows, gain = out_grad, skip_gain[None, :]
    if width != part:
        spread = lambda a: jnp.pad(
            a.reshape(a.shape[0], size, part), ((0, 0), (0, 0), (0, width - part))
        ).reshape(a.shape[0], whole)
        grad_rows, gain = spread(grad_rows), spread(gain)
    input_grad, filter_grad, skip_grad = run(
        functools.partial(last_kernel, size, length, width, clip_limit),
        "outputs",
        [
            jax.ShapeDtypeStruct((length, whole), f32),
            jax.ShapeDtypeStruct((length, whole), f32),
            jax.ShapeDtypeStruct((1, whole), f32),
        ],
    )(*filter_codes, *input_codes, grad_rows, gain)
    if width != part:
        gather = lambda a: a.reshape(a.shape[0], size, width)[:, :, :part].reshape(
            a.shape[0], chan_width
        )
        input_grad, filter_grad, skip_grad = gather(input_grad), gather(filter_grad), gather(skip_grad)
    return (input_grad, filter_grad, skip_grad[0])


def solution(mesh):
    return jax.shard_map(
        per_device,
        mesh=mesh,
        in_specs=(P("ctx", "chan"), P("ctx", "chan"), P("ctx", "chan"), P("chan")),
        out_specs=(P("ctx", "chan"), P("ctx", "chan"), P("chan")),
        check_vma=False,
    )
```

```python
import functools
import math

import jax
import jax.numpy as jnp
import numpy as np
from jax import lax
from jax.experimental import pallas as pl
from jax.experimental.pallas import tpu as pltpu
from jax.sharding import PartitionSpec as P

epsilon = 1e-06
octaves = 246
low_power = 120
top_code = 128 * octaves - 1
tail_rows = 16
first_flops = 4 * 10**9
second_flops = 2 * 10**10


def tables(length):
    odd = 2 * np.arange(length) + 1
    phase = odd[:, None] * np.arange(length)[None, :] % (4 * length)
    angles = np.pi * phase / (2 * length)
    forward = np.concatenate([np.cos(angles), -np.sin(angles)], axis=0)
    high = forward.astype(np.float32).astype(jnp.bfloat16)
    low = (forward - high.astype(np.float64)).astype(np.float32).astype(jnp.bfloat16)
    both = np.concatenate([high, low], axis=1)
    scale = np.float32(1.0 / length)
    back_high = (high.astype(np.float32).T * scale).astype(jnp.bfloat16)
    back_low = (low.astype(np.float32).T * scale).astype(jnp.bfloat16)
    return jnp.asarray(both), jnp.asarray(back_high), jnp.asarray(back_low)


def three_parts(value):
    high = value.astype(jnp.bfloat16).astype(jnp.float32)
    rest = value - high
    middle = rest.astype(jnp.bfloat16).astype(jnp.float32)
    return high, middle, rest - middle


def encode(values):
    peak = jnp.max(jnp.abs(values), axis=0, keepdims=True) * (1.0 + 2.0**-7)
    scale = jnp.maximum(peak.astype(jnp.bfloat16).astype(jnp.float32), 2.0**-110)
    units = values * (top_code / scale)
    code = jnp.minimum(jnp.floor(jnp.abs(units) + 0.5), float(top_code))
    octave = jnp.floor(code * (1.0 / 128))
    mantissa = 1.0 + (code - 128.0 * octave) * (1.0 / 128)
    carrier = mantissa * jnp.exp2(octave - float(low_power))
    return jnp.where(units < 0, -carrier, carrier).astype(jnp.bfloat16), scale


def decode(codes, scale):
    carrier = codes.astype(jnp.float32)
    size = jnp.abs(carrier)
    power = jnp.floor(jnp.log2(size) + 0.001)
    mantissa = jnp.floor(size * jnp.exp2(-power) * 128.0 + 0.5)
    units = (power + float(low_power - 1)) * 128.0 + mantissa
    return jnp.where(carrier < 0, -units, units) * (scale * (1.0 / top_code))


def tail_tile(first_row, rows, width):
    row_ids = lax.broadcasted_iota(jnp.int32, (tail_rows, width), 0)
    tile = jnp.zeros((tail_rows, width), jnp.float32)
    for i, row in enumerate(rows):
        tile = jnp.where(
            row_ids == first_row + i, jnp.broadcast_to(row, (tail_rows, width)), tile
        )
    return tile


def correlate_rows(pairs, others, size):
    results = []
    for p in range(size):
        real = imag = None
        for q in range(p, size):
            (gr, gi), (fr, fi) = pairs[q], others[q - p]
            real_term = gr * fr + gi * fi
            imag_term = gi * fr - gr * fi
            real = real_term if real is None else real + real_term
            imag = imag_term if imag is None else imag + imag_term
        results.append((real, imag))
    return results


def send_results(position, order, acc, back_high, back_low, emit):
    width = acc.shape[2]
    for i in range(0, len(order), 2):
        spec = jnp.concatenate([acc[position ^ order[i]], acc[position ^ order[i + 1]]], axis=1)
        high = spec.astype(jnp.bfloat16)
        low = (spec - high.astype(jnp.float32)).astype(jnp.bfloat16)
        dot = functools.partial(jnp.dot, preferred_element_type=jnp.float32)
        block = dot(back_high[...], high) + dot(back_high[...], low) + dot(back_low[...], high)
        emit(i, block[:, :width])
        emit(i + 1, block[:, width:])


def columns_kernel(chips, far, length, part, arrays, *refs):
    pairs, (own, other, taps, other_taps) = refs[:-4], refs[-4:]
    position = lax.axis_index("ctx")

    def put(out, row, j, k):
        columns = pl.ds(pl.multiple_of((position ^ k) * part, part), part)
        out[row : row + length] = arrays[j, :, columns]

    for i, chip in enumerate(chips):
        parts = 2 if i < far else 3
        here, there, there_row = (pairs[i], pairs[i], parts * length) if chip else (own, other, 0)
        for j in range(parts):
            put(here, j * length, j, 2 * chip)
            put(there, there_row + j * length, j, 2 * chip + 1)
    for i, chip in enumerate(chips[:far]):
        put(taps, i * length, 2, 2 * chip)
        put(other_taps, i * length, 2, 2 * chip + 1)


def pass_kernel(*refs):
    arrived, own, other, kept, passed = refs[:-4], *refs[-4:]
    row = 0
    for pair in arrived:
        rows = pair.shape[0] // 2
        kept[row : row + rows] = pair[:rows]
        passed[row : row + rows] = pair[rows:]
        row += rows
    kept[row:] = own[...]
    passed[row:] = other[...]


def first_kernel(order, length, places, *refs):
    size = len(order)
    both, back_high, back_low, codes_out, tails_out, pair_spec, squares, spec, acc = refs[-9:]
    width = spec.shape[2] // 2
    position = lax.axis_index("ctx")

    skip = jnp.zeros((1, width), jnp.float32)
    for i, k in enumerate(order):
        ref, row = places[i]
        grad, other = refs[ref][row : row + length], refs[ref][row + length : row + 2 * length]
        skip += jnp.sum(grad.astype(jnp.float32) * other.astype(jnp.float32), axis=0, keepdims=True)
        lanes = jnp.concatenate([grad, other], axis=1)
        spec[position ^ k] = jnp.dot(
            both[...], jnp.concatenate([lanes, lanes], axis=0), preferred_element_type=jnp.float32
        )

    flip = jnp.where(lax.broadcasted_iota(jnp.int32, (8, width), 0) % 2 == 0, 1.0, -1.0)

    def rows(r, carry):
        real_rows = pl.ds(pl.multiple_of(r * 8, 8), 8)
        imag_rows = pl.ds(pl.multiple_of(length + r * 8, 8), 8)
        grad = [(spec[q, real_rows, :width], spec[q, imag_rows, :width]) for q in range(size)]
        pairs = []
        for q in range(size):
            if q + 1 < size:
                real = grad[q][0] + flip * grad[q + 1][1]
                imag = grad[q][1] - flip * grad[q + 1][0]
            else:
                real, imag = grad[q]
            pair_spec[q, real_rows, :] = real
            pair_spec[q, imag_rows, :] = imag
            pairs.append((real, imag))
        others = [(spec[q, real_rows, width:], spec[q, imag_rows, width:]) for q in range(size)]
        for p, (real, imag) in enumerate(correlate_rows(pairs, others, size)):
            acc[p, real_rows, :] = real
            acc[p, imag_rows, :] = imag
        return carry

    lax.fori_loop(0, length // 8, rows, 0)
    skip_parts = three_parts(skip)
    squares[...] = jnp.zeros_like(squares)

    def emit(i, block):
        squares[...] += jnp.sum((block * block).reshape(length // 8, 8, width), axis=0)
        codes_out[i], scale = encode(block)
        tails_out[i] = tail_tile(0, (scale,) + skip_parts, width)

    send_results(position, order, acc, back_high, back_low, emit)


def second_kernel(order, length, places, *refs):
    size = len(order)
    both, back_high, back_low, pair_spec, codes_out, tails_out, spec, acc = refs[-8:]
    width = spec.shape[2]
    position = lax.axis_index("ctx")

    for i in range(0, size, 2):
        lanes = jnp.concatenate(
            [refs[ref][row : row + length] for ref, row in places[i : i + 2]], axis=1
        )
        both_specs = jnp.dot(
            both[...], jnp.concatenate([lanes, lanes], axis=0), preferred_element_type=jnp.float32
        )
        spec[position ^ order[i]] = both_specs[:, :width]
        spec[position ^ order[i + 1]] = both_specs[:, width:]

    def rows(r, carry):
        real_rows = pl.ds(pl.multiple_of(r * 8, 8), 8)
        imag_rows = pl.ds(pl.multiple_of(length + r * 8, 8), 8)
        pairs = [(pair_spec[q, real_rows, :], pair_spec[q, imag_rows, :]) for q in range(size)]
        others = [(spec[q, real_rows, :], spec[q, imag_rows, :]) for q in range(size)]
        for p, (real, imag) in enumerate(correlate_rows(pairs, others, size)):
            acc[p, real_rows, :] = real
            acc[p, imag_rows, :] = imag
        return carry

    lax.fori_loop(0, length // 8, rows, 0)

    def emit(i, block):
        codes_out[i], scale = encode(block)
        tails_out[i] = tail_tile(4, (scale,), width)

    send_results(position, order, acc, back_high, back_low, emit)


def message_kernel(size, length, sums, *refs):
    filter_codes, filter_tails, input_codes, input_tails = refs[:4]
    partial_squares, out = refs[4 : 4 + sums], refs[4 + sums :]
    squares = partial_squares[0][...]
    for other in partial_squares[1:]:
        squares += other[...]
    total = jnp.sum(jnp.sum(squares, axis=0, keepdims=True), axis=1, keepdims=True)
    width = squares.shape[1]
    total_rows = tail_tile(5, three_parts(jnp.broadcast_to(total, (1, width))), width)
    for i in range(size):
        out[i][:length] = filter_codes[i]
        out[i][length : 2 * length] = input_codes[i]
        tail = filter_tails[i] + input_tails[i] + total_rows
        out[i][2 * length :] = tail.astype(jnp.bfloat16)


def last_kernel(order, length, part, clip_limit, *refs):
    size = len(order)
    messages = refs[:size]
    grad, gain, input_grad, filter_grad, skip_grad = refs[size:]
    position = lax.axis_index("ctx")
    total = jnp.zeros((1, part), jnp.float32)
    for message in messages:
        tail = message[2 * length :].astype(jnp.float32)
        total += tail[5:6] + tail[6:7] + tail[7:8]
    factor = jnp.minimum(1.0, clip_limit / jnp.sqrt(total + epsilon))
    for k, message in zip(order, messages):
        columns = pl.ds(pl.multiple_of((position ^ k) * part, part), part)
        tail = message[2 * length :].astype(jnp.float32)
        filter_grad[:, columns] = decode(message[:length], tail[0:1]) * factor
        skip_grad[:, columns] = tail[1:2] + tail[2:3] + tail[3:4]
        input_grad[:, columns] = (
            decode(message[length : 2 * length], tail[4:5])
            + gain[:, columns] * grad[:, columns].astype(jnp.float32)
        )


def run(kernel, name, vmem_bytes, out_shape, scratch=(), flops=10**9, **specs):
    return pl.pallas_call(
        kernel,
        out_shape=out_shape,
        scratch_shapes=scratch,
        name=name,
        **specs,
        cost_estimate=pl.CostEstimate(flops=flops, bytes_accessed=0, transcendentals=0),
        compiler_params=pltpu.CompilerParams(vmem_limit_bytes=vmem_bytes),
    )


def per_device(inputs, filter_taps, out_grad, skip_gain):
    length, chan_width = inputs.shape
    size = lax.axis_size("ctx")
    columns = lax.axis_size("chan")
    part = chan_width // size
    width = -(-part // 128) * 128
    position = lax.axis_index("ctx")
    both, back_high, back_low = tables(length)
    f32, bf16 = jnp.float32, jnp.bfloat16
    chips = sorted(range(size // 2), key=lambda chip: (-chip.bit_length(), chip))
    order = [k for chip in chips for k in (2 * chip, 2 * chip + 1)]
    far = size // 4
    vmem_bytes = (8 + size) * 2**20

    def columns_for(array, k):
        block = lax.dynamic_slice_in_dim(array, (position ^ k) * part, part, 1)
        return jnp.pad(block, ((0, 0), (0, width - part)))

    def send(block, k):
        return lax.ppermute(block, "ctx", [(i, i ^ k) for i in range(size)])

    three = (out_grad, inputs, filter_taps)
    parts = [2] * far + [3] * (len(chips) - far)
    if width == part:
        blocks = [2 * n for n in parts[:-1]] + [3, 3, far, far]
        *pairs, own, other, taps, other_taps = run(
            functools.partial(columns_kernel, chips, far, length, part),
            "columns", vmem_bytes,
            [jax.ShapeDtypeStruct((n * length, width), bf16) for n in blocks],
        )(jnp.stack(three))
    else:
        cores = [
            [
                jnp.concatenate([columns_for(a, 2 * chip + core) for a in three[:n]])
                for chip, n in zip(chips, parts)
            ]
            for core in range(2)
        ]
        pairs = [jnp.concatenate(two) for two in zip(*cores)][:-1]
        own, other = cores[0][-1], cores[1][-1]
        taps, other_taps = (
            jnp.concatenate([columns_for(filter_taps, 2 * chip + core) for chip in chips[:far]])
            for core in range(2)
        )

    arrived = [send(pair, 2 * chip) for chip, pair in zip(chips, pairs)]
    kept, passed_on = run(
        pass_kernel,
        "passing", vmem_bytes,
        [jax.ShapeDtypeStruct((sum(parts) * length, width), bf16)] * 2,
    )(*arrived, own, other)
    passed_on = send(passed_on, 1)
    sibling_taps = send(other_taps, 1)
    sibling_taps, _ = lax.optimization_barrier((sibling_taps, arrived[-1]))
    arrived_taps = [
        send(
            jnp.concatenate(
                [held[i * length : (i + 1) * length] for held in (taps, sibling_taps)]
            ),
            2 * chip,
        )
        for i, chip in enumerate(chips[:far])
    ]
    first_places, second_places = [], []
    row = 0
    for i, n in enumerate(parts):
        first_places += [(0, row), (1, row)]
        taps_row = row + 2 * length
        second_places += [(i, 0), (i, length)] if i < far else [(far, taps_row), (far + 1, taps_row)]
        row += n * length
    first_arrived = [kept, passed_on]
    second_arrived = [*arrived_taps, kept, passed_on]

    codes, tails, pair_spec, squares = run(
        functools.partial(first_kernel, order, length, first_places),
        "filter_gradient", vmem_bytes,
        [
            jax.ShapeDtypeStruct((size, length, width), bf16),
            jax.ShapeDtypeStruct((size, tail_rows, width), f32),
            jax.ShapeDtypeStruct((size, 2 * length, width), f32),
            jax.ShapeDtypeStruct((8, width), f32),
        ],
        [
            pltpu.VMEM((size, 2 * length, 2 * width), f32),
            pltpu.VMEM((size, 2 * length, width), f32),
        ],
        flops=first_flops,
    )(*first_arrived, both, back_high, back_low)
    all_squares = [
        squares if k == 0 else lax.ppermute(squares, "chan", [(i, i ^ k) for i in range(columns)])
        for k in range(columns)
    ]
    input_codes, input_tails = run(
        functools.partial(second_kernel, order, length, second_places),
        "input_gradient", vmem_bytes,
        [
            jax.ShapeDtypeStruct((size, length, width), bf16),
            jax.ShapeDtypeStruct((size, tail_rows, width), f32),
        ],
        [
            pltpu.VMEM((size, 2 * length, width), f32),
            pltpu.VMEM((size, 2 * length, width), f32),
        ],
        flops=second_flops,
    )(*second_arrived, both, back_high, back_low, pair_spec)
    messages = run(
        functools.partial(message_kernel, size, length, columns),
        "messages", vmem_bytes,
        [jax.ShapeDtypeStruct((2 * length + tail_rows, width), bf16)] * size,
    )(codes, tails, input_codes, input_tails, *all_squares)
    messages = [send(message, k) if k else message for k, message in zip(order, messages)]

    clip_limit = 0.25 * math.sqrt(length * size * chan_width * columns)
    whole = size * width
    grad_rows, gain = out_grad, skip_gain[None, :]
    if width != part:
        spread = lambda a: jnp.pad(
            a.reshape(a.shape[0], size, part), ((0, 0), (0, 0), (0, width - part))
        ).reshape(a.shape[0], whole)
        grad_rows, gain = spread(grad_rows), spread(gain)
    input_grad, filter_grad, skip_grad = run(
        functools.partial(last_kernel, order, length, width, clip_limit),
        "outputs", vmem_bytes,
        [
            jax.ShapeDtypeStruct((length, whole), f32),
            jax.ShapeDtypeStruct((length, whole), f32),
            jax.ShapeDtypeStruct((1, whole), f32),
        ],
    )(*messages, grad_rows, gain)
    if width != part:
        gather = lambda a: a.reshape(a.shape[0], size, width)[:, :, :part].reshape(
            a.shape[0], chan_width
        )
        input_grad, filter_grad, skip_grad = gather(input_grad), gather(filter_grad), gather(skip_grad)
    return (input_grad, filter_grad, skip_grad[0])


def solution(mesh):
    return jax.shard_map(
        per_device,
        mesh=mesh,
        in_specs=(P("ctx", "chan"), P("ctx", "chan"), P("ctx", "chan"), P("chan")),
        out_specs=(P("ctx", "chan"), P("ctx", "chan"), P("chan")),
        check_vma=False,
    )
```

```python
import functools
import math

import jax
import jax.numpy as jnp
import numpy as np
from jax import lax
from jax.experimental import pallas as pl
from jax.experimental.pallas import tpu as pltpu
from jax.sharding import PartitionSpec as P

epsilon = 1e-06
octaves = 246
low_power = 120
top_code = 128 * octaves - 1
tail_rows = 16
first_flops = 4 * 10**9
second_flops = 2 * 10**10


def tables(length):
    odd = 2 * np.arange(length) + 1
    phase = odd[:, None] * np.arange(length)[None, :] % (4 * length)
    angles = np.pi * phase / (2 * length)
    forward = np.concatenate([np.cos(angles), -np.sin(angles)], axis=0)
    high = forward.astype(np.float32).astype(jnp.bfloat16)
    low = (forward - high.astype(np.float64)).astype(np.float32).astype(jnp.bfloat16)
    both = np.concatenate([high, low], axis=1)
    scale = np.float32(1.0 / length)
    back_high = (high.astype(np.float32).T * scale).astype(jnp.bfloat16)
    back_low = (low.astype(np.float32).T * scale).astype(jnp.bfloat16)
    return jnp.asarray(both), jnp.asarray(back_high), jnp.asarray(back_low)


def three_parts(value):
    high = value.astype(jnp.bfloat16).astype(jnp.float32)
    rest = value - high
    middle = rest.astype(jnp.bfloat16).astype(jnp.float32)
    return high, middle, rest - middle


def encode(values):
    peak = jnp.max(jnp.abs(values), axis=0, keepdims=True) * (1.0 + 2.0**-7)
    scale = jnp.maximum(peak.astype(jnp.bfloat16).astype(jnp.float32), 2.0**-110)
    units = values * (top_code / scale)
    code = jnp.minimum(jnp.floor(jnp.abs(units) + 0.5), float(top_code))
    octave = jnp.floor(code * (1.0 / 128))
    mantissa = 1.0 + (code - 128.0 * octave) * (1.0 / 128)
    carrier = mantissa * jnp.exp2(octave - float(low_power))
    return jnp.where(units < 0, -carrier, carrier).astype(jnp.bfloat16), scale


def decode(codes, scale):
    carrier = codes.astype(jnp.float32)
    size = jnp.abs(carrier)
    power = jnp.floor(jnp.log2(size) + 0.001)
    mantissa = jnp.floor(size * jnp.exp2(-power) * 128.0 + 0.5)
    units = (power + float(low_power - 1)) * 128.0 + mantissa
    return jnp.where(carrier < 0, -units, units) * (scale * (1.0 / top_code))


def tail_tile(first_row, rows, width):
    row_ids = lax.broadcasted_iota(jnp.int32, (tail_rows, width), 0)
    tile = jnp.zeros((tail_rows, width), jnp.float32)
    for i, row in enumerate(rows):
        tile = jnp.where(
            row_ids == first_row + i, jnp.broadcast_to(row, (tail_rows, width)), tile
        )
    return tile


def correlate_rows(pairs, others, size):
    results = []
    for p in range(size):
        real = imag = None
        for q in range(p, size):
            (gr, gi), (fr, fi) = pairs[q], others[q - p]
            real_term = gr * fr + gi * fi
            imag_term = gi * fr - gr * fi
            real = real_term if real is None else real + real_term
            imag = imag_term if imag is None else imag + imag_term
        results.append((real, imag))
    return results


def send_results(position, order, acc, back_high, back_low, emit):
    width = acc.shape[2]
    for i in range(0, len(order), 2):
        spec = jnp.concatenate([acc[position ^ order[i]], acc[position ^ order[i + 1]]], axis=1)
        high = spec.astype(jnp.bfloat16)
        low = (spec - high.astype(jnp.float32)).astype(jnp.bfloat16)
        dot = functools.partial(jnp.dot, preferred_element_type=jnp.float32)
        block = dot(back_high[...], high) + dot(back_high[...], low) + dot(back_low[...], high)
        emit(i, block[:, :width])
        emit(i + 1, block[:, width:])


def columns_kernel(chips, far, length, part, arrays, *refs):
    direct, pairs, (own, other, taps, other_taps) = refs[: 2 * far], refs[2 * far : -4], refs[-4:]
    position = lax.axis_index("ctx")

    def put(out, row, j, k):
        columns = pl.ds(pl.multiple_of((position ^ k) * part, part), part)
        out[row : row + length] = arrays[j, :, columns]

    for i, chip in enumerate(chips[:far]):
        for j in range(2):
            put(direct[2 * i], j * length, j, 2 * chip)
            put(direct[2 * i + 1], j * length, j, 2 * chip + 1)
        put(taps, i * length, 2, 2 * chip)
        put(other_taps, i * length, 2, 2 * chip + 1)
    for i, chip in enumerate(chips[far:]):
        here, there, there_row = (pairs[i], pairs[i], 3 * length) if chip else (own, other, 0)
        for j in range(3):
            put(here, j * length, j, 2 * chip)
            put(there, there_row + j * length, j, 2 * chip + 1)


def pass_kernel(*refs):
    arrived, (own, other), tables, (kept, passed), held = refs[:-10], *(
        refs[i:j] for i, j in ((-10, -8), (-8, -5), (-5, -3), (-3, None))
    )
    for table, place in zip(tables, held):
        place[...] = table[...]
    row = 0
    for pair in arrived:
        rows = pair.shape[0] // 2
        kept[row : row + rows] = pair[:rows]
        passed[row : row + rows] = pair[rows:]
        row += rows
    kept[row:] = own[...]
    passed[row:] = other[...]


def first_kernel(order, length, places, *refs):
    size = len(order)
    both, back_high, back_low, codes_out, tails_out, pair_spec, squares, spec, acc = refs[-9:]
    width = spec.shape[2] // 2
    position = lax.axis_index("ctx")

    skip = jnp.zeros((1, width), jnp.float32)
    for i, k in enumerate(order):
        ref, row = places[i]
        grad, other = refs[ref][row : row + length], refs[ref][row + length : row + 2 * length]
        skip += jnp.sum(grad.astype(jnp.float32) * other.astype(jnp.float32), axis=0, keepdims=True)
        lanes = jnp.concatenate([grad, other], axis=1)
        spec[position ^ k] = jnp.dot(
            both[...], jnp.concatenate([lanes, lanes], axis=0), preferred_element_type=jnp.float32
        )

    flip = jnp.where(lax.broadcasted_iota(jnp.int32, (8, width), 0) % 2 == 0, 1.0, -1.0)

    def rows(r, carry):
        real_rows = pl.ds(pl.multiple_of(r * 8, 8), 8)
        imag_rows = pl.ds(pl.multiple_of(length + r * 8, 8), 8)
        grad = [(spec[q, real_rows, :width], spec[q, imag_rows, :width]) for q in range(size)]
        pairs = []
        for q in range(size):
            if q + 1 < size:
                real = grad[q][0] + flip * grad[q + 1][1]
                imag = grad[q][1] - flip * grad[q + 1][0]
            else:
                real, imag = grad[q]
            pair_spec[q, real_rows, :] = real
            pair_spec[q, imag_rows, :] = imag
            pairs.append((real, imag))
        others = [(spec[q, real_rows, width:], spec[q, imag_rows, width:]) for q in range(size)]
        for p, (real, imag) in enumerate(correlate_rows(pairs, others, size)):
            acc[p, real_rows, :] = real
            acc[p, imag_rows, :] = imag
        return carry

    lax.fori_loop(0, length // 8, rows, 0)
    skip_parts = three_parts(skip)
    squares[...] = jnp.zeros_like(squares)

    def emit(i, block):
        squares[...] += jnp.sum((block * block).reshape(length // 8, 8, width), axis=0)
        codes_out[i], scale = encode(block)
        tails_out[i] = tail_tile(0, (scale,) + skip_parts, width)

    send_results(position, order, acc, back_high, back_low, emit)


def second_kernel(order, length, places, *refs):
    size = len(order)
    both, back_high, back_low, pair_spec, codes_out, tails_out, spec, acc = refs[-8:]
    width = spec.shape[2]
    position = lax.axis_index("ctx")

    for i in range(0, size, 2):
        lanes = jnp.concatenate(
            [refs[ref][row : row + length] for ref, row in places[i : i + 2]], axis=1
        )
        both_specs = jnp.dot(
            both[...], jnp.concatenate([lanes, lanes], axis=0), preferred_element_type=jnp.float32
        )
        spec[position ^ order[i]] = both_specs[:, :width]
        spec[position ^ order[i + 1]] = both_specs[:, width:]

    def rows(r, carry):
        real_rows = pl.ds(pl.multiple_of(r * 8, 8), 8)
        imag_rows = pl.ds(pl.multiple_of(length + r * 8, 8), 8)
        pairs = [(pair_spec[q, real_rows, :], pair_spec[q, imag_rows, :]) for q in range(size)]
        others = [(spec[q, real_rows, :], spec[q, imag_rows, :]) for q in range(size)]
        for p, (real, imag) in enumerate(correlate_rows(pairs, others, size)):
            acc[p, real_rows, :] = real
            acc[p, imag_rows, :] = imag
        return carry

    lax.fori_loop(0, length // 8, rows, 0)

    def emit(i, block):
        codes_out[i], scale = encode(block)
        tails_out[i] = tail_tile(4, (scale,), width)

    send_results(position, order, acc, back_high, back_low, emit)


def message_kernel(size, length, sums, *refs):
    filter_codes, filter_tails, input_codes, input_tails = refs[:4]
    partial_squares, out = refs[4 : 4 + sums], refs[4 + sums :]
    squares = partial_squares[0][...]
    for other in partial_squares[1:]:
        squares += other[...]
    total = jnp.sum(jnp.sum(squares, axis=0, keepdims=True), axis=1, keepdims=True)
    width = squares.shape[1]
    total_rows = tail_tile(5, three_parts(jnp.broadcast_to(total, (1, width))), width)
    for i in range(size):
        out[i][:length] = filter_codes[i]
        out[i][length : 2 * length] = input_codes[i]
        tail = filter_tails[i] + input_tails[i] + total_rows
        out[i][2 * length :] = tail.astype(jnp.bfloat16)


def last_kernel(order, length, part, clip_limit, *refs):
    size = len(order)
    messages = refs[:size]
    grad, gain, input_grad, filter_grad, skip_grad = refs[size:]
    position = lax.axis_index("ctx")
    total = jnp.zeros((1, part), jnp.float32)
    for message in messages:
        tail = message[2 * length :].astype(jnp.float32)
        total += tail[5:6] + tail[6:7] + tail[7:8]
    factor = jnp.minimum(1.0, clip_limit / jnp.sqrt(total + epsilon))
    for k, message in zip(order, messages):
        columns = pl.ds(pl.multiple_of((position ^ k) * part, part), part)
        tail = message[2 * length :].astype(jnp.float32)
        filter_grad[:, columns] = decode(message[:length], tail[0:1]) * factor
        skip_grad[:, columns] = tail[1:2] + tail[2:3] + tail[3:4]
        input_grad[:, columns] = (
            decode(message[length : 2 * length], tail[4:5])
            + gain[:, columns] * grad[:, columns].astype(jnp.float32)
        )


def run(kernel, name, vmem_bytes, out_shape, scratch=(), flops=10**9, **specs):
    return pl.pallas_call(
        kernel,
        out_shape=out_shape,
        scratch_shapes=scratch,
        name=name,
        **specs,
        cost_estimate=pl.CostEstimate(flops=flops, bytes_accessed=0, transcendentals=0),
        compiler_params=pltpu.CompilerParams(vmem_limit_bytes=vmem_bytes),
    )


def per_device(inputs, filter_taps, out_grad, skip_gain):
    length, chan_width = inputs.shape
    size = lax.axis_size("ctx")
    columns = lax.axis_size("chan")
    part = chan_width // size
    width = -(-part // 128) * 128
    position = lax.axis_index("ctx")
    both, back_high, back_low = tables(length)
    f32, bf16 = jnp.float32, jnp.bfloat16
    chips = sorted(range(size // 2), key=lambda chip: (-chip.bit_length(), chip))
    order = [k for chip in chips for k in (2 * chip, 2 * chip + 1)]
    far = size // 4
    vmem_bytes = (8 + size) * 2**20

    def columns_for(array, k):
        block = lax.dynamic_slice_in_dim(array, (position ^ k) * part, part, 1)
        return jnp.pad(block, ((0, 0), (0, width - part)))

    def send(block, k):
        return lax.ppermute(block, "ctx", [(i, i ^ k) for i in range(size)])

    three = (out_grad, inputs, filter_taps)
    near = len(chips) - far
    if width == part:
        blocks = [2] * (2 * far) + [6] * (near - 1) + [3, 3, far, far]
        *sent, own, other, taps, other_taps = run(
            functools.partial(columns_kernel, chips, far, length, part),
            "columns", vmem_bytes,
            [jax.ShapeDtypeStruct((n * length, width), bf16) for n in blocks],
        )(jnp.stack(three))
    else:
        sent = [
            jnp.concatenate([columns_for(a, k) for a in three[:2]]) for k in order[: 2 * far]
        ] + [
            jnp.concatenate([columns_for(a, 2 * chip + core) for core in range(2) for a in three])
            for chip in chips[far:-1]
        ]
        own, other = (jnp.concatenate([columns_for(a, core) for a in three]) for core in range(2))
        taps, other_taps = (
            jnp.concatenate([columns_for(filter_taps, 2 * chip + core) for chip in chips[:far]])
            for core in range(2)
        )

    partners = order[: 2 * far] + [2 * chip for chip in chips[far:-1]]
    arrived = [send(block, k) for k, block in zip(partners, sent)]
    kept, passed_on, both, back_high, back_low = run(
        pass_kernel,
        "passing", vmem_bytes,
        [jax.ShapeDtypeStruct((near * 3 * length, width), bf16)] * 2
        + [jax.ShapeDtypeStruct(t.shape, t.dtype) for t in (both, back_high, back_low)],
    )(*arrived[2 * far :], own, other, both, back_high, back_low)
    passed_on = send(passed_on, 1)
    other_taps, _ = lax.optimization_barrier((other_taps, arrived[-1]))
    sibling_taps = send(other_taps, 1)
    sibling_taps, passed_on = lax.optimization_barrier((sibling_taps, passed_on))
    arrived_taps = [
        send(
            jnp.concatenate(
                [held[i * length : (i + 1) * length] for held in (taps, sibling_taps)]
            ),
            2 * chip,
        )
        for i, chip in enumerate(chips[:far])
    ]
    first_arrived = [*arrived[: 2 * far], kept, passed_on]
    first_places = [(i, 0) for i in range(2 * far)]
    second_arrived = [*arrived_taps, kept, passed_on]
    second_places = [(i, row) for i in range(far) for row in (0, length)]
    for row in range(0, near * 3 * length, 3 * length):
        first_places += [(2 * far, row), (2 * far + 1, row)]
        second_places += [(far, row + 2 * length), (far + 1, row + 2 * length)]

    codes, tails, pair_spec, squares = run(
        functools.partial(first_kernel, order, length, first_places),
        "filter_gradient", vmem_bytes,
        [
            jax.ShapeDtypeStruct((size, length, width), bf16),
            jax.ShapeDtypeStruct((size, tail_rows, width), f32),
            jax.ShapeDtypeStruct((size, 2 * length, width), f32),
            jax.ShapeDtypeStruct((8, width), f32),
        ],
        [
            pltpu.VMEM((size, 2 * length, 2 * width), f32),
            pltpu.VMEM((size, 2 * length, width), f32),
        ],
        flops=first_flops,
    )(*first_arrived, both, back_high, back_low)
    all_squares = [
        squares if k == 0 else lax.ppermute(squares, "chan", [(i, i ^ k) for i in range(columns)])
        for k in range(columns)
    ]
    input_codes, input_tails = run(
        functools.partial(second_kernel, order, length, second_places),
        "input_gradient", vmem_bytes,
        [
            jax.ShapeDtypeStruct((size, length, width), bf16),
            jax.ShapeDtypeStruct((size, tail_rows, width), f32),
        ],
        [
            pltpu.VMEM((size, 2 * length, width), f32),
            pltpu.VMEM((size, 2 * length, width), f32),
        ],
        flops=second_flops,
    )(*second_arrived, both, back_high, back_low, pair_spec)
    messages = run(
        functools.partial(message_kernel, size, length, columns),
        "messages", vmem_bytes,
        [jax.ShapeDtypeStruct((2 * length + tail_rows, width), bf16)] * size,
    )(codes, tails, input_codes, input_tails, *all_squares)
    messages = {k: send(message, k) if k else message for k, message in zip(order, messages)}
    turns = chips[: far // 2] + chips[far:-1] + chips[far // 2 : far] + [0]
    turns = [k for chip in turns for k in (2 * chip, 2 * chip + 1)]

    clip_limit = 0.25 * math.sqrt(length * size * chan_width * columns)
    whole = size * width
    grad_rows, gain = out_grad, skip_gain[None, :]
    if width != part:
        spread = lambda a: jnp.pad(
            a.reshape(a.shape[0], size, part), ((0, 0), (0, 0), (0, width - part))
        ).reshape(a.shape[0], whole)
        grad_rows, gain = spread(grad_rows), spread(gain)
    input_grad, filter_grad, skip_grad = run(
        functools.partial(last_kernel, turns, length, width, clip_limit),
        "outputs", vmem_bytes,
        [
            jax.ShapeDtypeStruct((length, whole), f32),
            jax.ShapeDtypeStruct((length, whole), f32),
            jax.ShapeDtypeStruct((1, whole), f32),
        ],
    )(*[messages[k] for k in turns], grad_rows, gain)
    if width != part:
        gather = lambda a: a.reshape(a.shape[0], size, width)[:, :, :part].reshape(
            a.shape[0], chan_width
        )
        input_grad, filter_grad, skip_grad = gather(input_grad), gather(filter_grad), gather(skip_grad)
    return (input_grad, filter_grad, skip_grad[0])


def solution(mesh):
    return jax.shard_map(
        per_device,
        mesh=mesh,
        in_specs=(P("ctx", "chan"), P("ctx", "chan"), P("ctx", "chan"), P("chan")),
        out_specs=(P("ctx", "chan"), P("ctx", "chan"), P("chan")),
        check_vma=False,
    )
```

```python
import functools
import math

import jax
import jax.numpy as jnp
import numpy as np
from jax import lax
from jax.experimental import pallas as pl
from jax.experimental.pallas import tpu as pltpu
from jax.sharding import PartitionSpec as P

epsilon = 1e-06
octaves = 246
low_power = 120
top_code = 128 * octaves - 1
tail_rows = 16
first_flops = 4 * 10**9
second_flops = 2 * 10**10


def tables(length):
    odd = 2 * np.arange(length) + 1
    phase = odd[:, None] * np.arange(length)[None, :] % (4 * length)
    angles = np.pi * phase / (2 * length)
    forward = np.concatenate([np.cos(angles), -np.sin(angles)], axis=0)
    high = forward.astype(np.float32).astype(jnp.bfloat16)
    low = (forward - high.astype(np.float64)).astype(np.float32).astype(jnp.bfloat16)
    both = np.concatenate([high, low], axis=1)
    scale = np.float32(1.0 / length)
    back_high = (high.astype(np.float32).T * scale).astype(jnp.bfloat16)
    back_low = (low.astype(np.float32).T * scale).astype(jnp.bfloat16)
    return jnp.asarray(both), jnp.asarray(back_high), jnp.asarray(back_low)


def three_parts(value):
    high = value.astype(jnp.bfloat16).astype(jnp.float32)
    rest = value - high
    middle = rest.astype(jnp.bfloat16).astype(jnp.float32)
    return high, middle, rest - middle


def encode(values):
    peak = jnp.max(jnp.abs(values), axis=0, keepdims=True) * (1.0 + 2.0**-7)
    scale = jnp.maximum(peak.astype(jnp.bfloat16).astype(jnp.float32), 2.0**-110)
    size = jnp.abs(values) * (top_code / 128.0 / scale)
    octave = jnp.floor(size)
    carrier = (size - octave + 1.0) * jnp.exp2(octave - float(low_power))
    return jnp.where(values < 0, -carrier, carrier).astype(jnp.bfloat16), scale


def decode(codes, scale):
    carrier = codes.astype(jnp.float32)
    size = jnp.abs(carrier)
    power = jnp.floor(jnp.log2(size) + 0.001)
    octaves_up = size * jnp.exp2(-power) + (power + float(low_power - 1))
    scale *= 128.0 / top_code
    return octaves_up * jnp.where(carrier < 0, -scale, scale)


def tail_tile(first_row, rows, width):
    row_ids = lax.broadcasted_iota(jnp.int32, (tail_rows, width), 0)
    tile = jnp.zeros((tail_rows, width), jnp.float32)
    for i, row in enumerate(rows):
        tile = jnp.where(
            row_ids == first_row + i, jnp.broadcast_to(row, (tail_rows, width)), tile
        )
    return tile


def correlate_rows(pairs, others, size):
    sums = [real + imag for real, imag in pairs]
    turned = [(real, real - imag, real + imag) for real, imag in others]
    results = []
    for p in range(size):
        shared = first = second = None
        for q in range(p, size):
            real, less, more = turned[q - p]
            terms = sums[q] * real, pairs[q][1] * less, pairs[q][0] * more
            if q > p:
                terms = shared + terms[0], first + terms[1], second + terms[2]
            shared, first, second = terms
        results.append((shared - first, shared - second))
    return results


def send_results(position, order, acc, back_high, back_low, emit):
    width = acc.shape[2]
    for i in range(0, len(order), 2):
        spec = jnp.concatenate([acc[position ^ order[i]], acc[position ^ order[i + 1]]], axis=1)
        high = spec.astype(jnp.bfloat16)
        low = (spec - high.astype(jnp.float32)).astype(jnp.bfloat16)
        dot = functools.partial(jnp.dot, preferred_element_type=jnp.float32)
        block = dot(back_high[...], high) + dot(back_high[...], low) + dot(back_low[...], high)
        emit(i, block[:, :width])
        emit(i + 1, block[:, width:])


def columns_kernel(chips, direct, length, part, arrays, *refs):
    blocks, rest = refs[:-2], refs[-2:]
    position = lax.axis_index("ctx")

    def put(out, row, j, k):
        columns = pl.ds(pl.multiple_of((position ^ k) * part, part), part)
        out[row : row + length] = arrays[j, :, columns]

    for core in range(2):
        row = 0
        for i, chip in enumerate(chips):
            for j in range(3):
                if i < direct and j < 2:
                    put(blocks[2 * i + core], j * length, j, 2 * chip + core)
                else:
                    put(rest[core], row, j, 2 * chip + core)
                    row += length


def taps_kernel(rows, length, mine, sibling, *refs):
    tables, messages, held = refs[:3], refs[3:-3], refs[-3:]
    for table, place in zip(tables, held):
        place[...] = table[...]
    for row, message in zip(rows, messages):
        message[:length] = mine[row : row + length]
        message[length:] = sibling[row : row + length]


def first_kernel(order, length, places, *refs):
    size = len(order)
    both, back_high, back_low, codes_out, tails_out, pair_spec, squares, spec, acc = refs[-9:]
    width = spec.shape[2] // 2
    position = lax.axis_index("ctx")

    skip = jnp.zeros((1, width), jnp.float32)
    for i, k in enumerate(order):
        ref, row = places[i]
        grad, other = refs[ref][row : row + length], refs[ref][row + length : row + 2 * length]
        skip += jnp.sum(grad.astype(jnp.float32) * other.astype(jnp.float32), axis=0, keepdims=True)
        lanes = jnp.concatenate([grad, other], axis=1)
        spec[position ^ k] = jnp.dot(
            both[...], jnp.concatenate([lanes, lanes], axis=0), preferred_element_type=jnp.float32
        )

    flip = jnp.where(lax.broadcasted_iota(jnp.int32, (8, width), 0) % 2 == 0, 1.0, -1.0)

    def rows(r, carry):
        real_rows = pl.ds(pl.multiple_of(r * 8, 8), 8)
        imag_rows = pl.ds(pl.multiple_of(length + r * 8, 8), 8)
        grad = [(spec[q, real_rows, :width], spec[q, imag_rows, :width]) for q in range(size)]
        pairs = []
        for q in range(size):
            if q + 1 < size:
                real = grad[q][0] + flip * grad[q + 1][1]
                imag = grad[q][1] - flip * grad[q + 1][0]
            else:
                real, imag = grad[q]
            pair_spec[q, real_rows, :] = real
            pair_spec[q, imag_rows, :] = imag
            pairs.append((real, imag))
        others = [(spec[q, real_rows, width:], spec[q, imag_rows, width:]) for q in range(size)]
        for p, (real, imag) in enumerate(correlate_rows(pairs, others, size)):
            acc[p, real_rows, :] = real
            acc[p, imag_rows, :] = imag
        return carry

    lax.fori_loop(0, length // 8, rows, 0)
    skip_parts = three_parts(skip)
    squares[...] = jnp.zeros_like(squares)

    def emit(i, block):
        squares[...] += jnp.sum((block * block).reshape(length // 8, 8, width), axis=0)
        codes_out[i], scale = encode(block)
        tails_out[i] = tail_tile(0, (scale,) + skip_parts, width)

    send_results(position, order, acc, back_high, back_low, emit)


def second_kernel(order, length, places, *refs):
    size = len(order)
    both, back_high, back_low, pair_spec, codes_out, tails_out, spec, acc = refs[-8:]
    width = spec.shape[2]
    position = lax.axis_index("ctx")

    for i in range(0, size, 2):
        lanes = jnp.concatenate(
            [refs[ref][row : row + length] for ref, row in places[i : i + 2]], axis=1
        )
        both_specs = jnp.dot(
            both[...], jnp.concatenate([lanes, lanes], axis=0), preferred_element_type=jnp.float32
        )
        spec[position ^ order[i]] = both_specs[:, :width]
        spec[position ^ order[i + 1]] = both_specs[:, width:]

    def rows(r, carry):
        real_rows = pl.ds(pl.multiple_of(r * 8, 8), 8)
        imag_rows = pl.ds(pl.multiple_of(length + r * 8, 8), 8)
        pairs = [(pair_spec[q, real_rows, :], pair_spec[q, imag_rows, :]) for q in range(size)]
        others = [(spec[q, real_rows, :], spec[q, imag_rows, :]) for q in range(size)]
        for p, (real, imag) in enumerate(correlate_rows(pairs, others, size)):
            acc[p, real_rows, :] = real
            acc[p, imag_rows, :] = imag
        return carry

    lax.fori_loop(0, length // 8, rows, 0)

    def emit(i, block):
        codes_out[i], scale = encode(block)
        tails_out[i] = tail_tile(4, (scale,), width)

    send_results(position, order, acc, back_high, back_low, emit)


def message_kernel(size, length, sums, *refs):
    filter_codes, filter_tails, input_codes, input_tails = refs[:4]
    partial_squares, out = refs[4 : 4 + sums], refs[4 + sums :]
    squares = partial_squares[0][...]
    for other in partial_squares[1:]:
        squares += other[...]
    total = jnp.sum(jnp.sum(squares, axis=0, keepdims=True), axis=1, keepdims=True)
    width = squares.shape[1]
    total_rows = tail_tile(5, three_parts(jnp.broadcast_to(total, (1, width))), width)
    for i in range(size):
        out[i][:length] = filter_codes[i]
        out[i][length : 2 * length] = input_codes[i]
        tail = filter_tails[i] + input_tails[i] + total_rows
        out[i][2 * length :] = tail.astype(jnp.bfloat16)


def last_kernel(order, length, part, clip_limit, *refs):
    size = len(order)
    messages = refs[:size]
    grad, gain, input_grad, filter_grad, skip_grad = refs[size:]
    position = lax.axis_index("ctx")
    total = jnp.zeros((1, part), jnp.float32)
    for message in messages:
        tail = message[2 * length :].astype(jnp.float32)
        total += tail[5:6] + tail[6:7] + tail[7:8]
    factor = jnp.minimum(1.0, clip_limit / jnp.sqrt(total + epsilon))
    for k, message in zip(order, messages):
        columns = pl.ds(pl.multiple_of((position ^ k) * part, part), part)
        tail = message[2 * length :].astype(jnp.float32)
        filter_grad[:, columns] = decode(message[:length], tail[0:1]) * factor
        skip_grad[:, columns] = tail[1:2] + tail[2:3] + tail[3:4]
        input_grad[:, columns] = (
            decode(message[length : 2 * length], tail[4:5])
            + gain[:, columns] * grad[:, columns].astype(jnp.float32)
        )


def run(kernel, name, vmem_bytes, out_shape, scratch=(), flops=10**9, **specs):
    return pl.pallas_call(
        kernel,
        out_shape=out_shape,
        scratch_shapes=scratch,
        name=name,
        **specs,
        cost_estimate=pl.CostEstimate(flops=flops, bytes_accessed=0, transcendentals=0),
        compiler_params=pltpu.CompilerParams(vmem_limit_bytes=vmem_bytes),
    )


def per_device(inputs, filter_taps, out_grad, skip_gain):
    length, chan_width = inputs.shape
    size = lax.axis_size("ctx")
    columns = lax.axis_size("chan")
    part = chan_width // size
    width = -(-part // 128) * 128
    position = lax.axis_index("ctx")
    both, back_high, back_low = tables(length)
    f32, bf16 = jnp.float32, jnp.bfloat16
    chips = sorted(range(size // 2), key=lambda chip: (-chip.bit_length(), chip))
    order = [k for chip in chips for k in (2 * chip, 2 * chip + 1)]
    far = size // 4
    vmem_bytes = (8 + size) * 2**20

    def columns_for(array, k):
        block = lax.dynamic_slice_in_dim(array, (position ^ k) * part, part, 1)
        return jnp.pad(block, ((0, 0), (0, width - part)))

    def send(block, k):
        return lax.ppermute(block, "ctx", [(i, i ^ k) for i in range(size)])

    three = (out_grad, inputs, filter_taps)
    direct = size // 8
    rest_rows = (3 * len(chips) - 2 * direct) * length
    if width == part:
        *blocks, mine, others = run(
            functools.partial(columns_kernel, chips, direct, length, part),
            "columns", vmem_bytes,
            [jax.ShapeDtypeStruct((2 * length, width), bf16)] * (2 * direct)
            + [jax.ShapeDtypeStruct((rest_rows, width), bf16)] * 2,
        )(jnp.stack(three))
    else:
        blocks = [jnp.concatenate([columns_for(a, k) for a in three[:2]]) for k in order[: 2 * direct]]
        mine, others = (
            jnp.concatenate(
                [
                    columns_for(a, 2 * chip + core)
                    for i, chip in enumerate(chips)
                    for a in (three[2:] if i < direct else three)
                ]
            )
            for core in range(2)
        )

    sibling = send(others, 1)
    arrived = [send(block, k) for k, block in zip(order, blocks)]
    first_places = [(i, 0) for i in range(2 * direct)]
    taps_rows = [i * length for i in range(direct)]
    row = direct * length
    near_places = []
    for i, chip in enumerate(chips[direct:-1]):
        here = len(arrived)
        rows = (2 if i < far - direct else 3) * length
        pair = jnp.concatenate([held[row : row + rows] for held in (mine, sibling)])
        first_places += [(here, 0), (here, rows)]
        arrived.append(send(pair, 2 * chip))
        if i < far - direct:
            taps_rows.append(row + 2 * length)
        else:
            near_places += [(here, 2 * length), (here, 5 * length)]
        row += 3 * length
    first_places += [(len(arrived), row), (len(arrived) + 1, row)]
    first_arrived = [*arrived, mine, sibling]
    later = lax.optimization_barrier((mine, sibling, *arrived[: 2 * direct]))[:2]
    *tap_messages, both, back_high, back_low = run(
        functools.partial(taps_kernel, taps_rows, length),
        "taps", vmem_bytes,
        [jax.ShapeDtypeStruct((2 * length, width), bf16)] * len(taps_rows)
        + [jax.ShapeDtypeStruct(t.shape, t.dtype) for t in (both, back_high, back_low)],
    )(*later, both, back_high, back_low)
    arrived_taps = [send(block, 2 * chip) for chip, block in zip(chips, tap_messages)]
    second_places = [(i, half) for i in range(far) for half in (0, length)]
    second_places += [(ref - 2 * direct - (far - direct) + far, at) for ref, at in near_places]
    second_arrived = [*arrived_taps, *arrived[direct + far :], mine, sibling]
    second_places += [(len(second_arrived) - 2 + i, row + 2 * length) for i in range(2)]

    codes, tails, pair_spec, squares = run(
        functools.partial(first_kernel, order, length, first_places),
        "filter_gradient", vmem_bytes,
        [
            jax.ShapeDtypeStruct((size, length, width), bf16),
            jax.ShapeDtypeStruct((size, tail_rows, width), f32),
            jax.ShapeDtypeStruct((size, 2 * length, width), f32),
            jax.ShapeDtypeStruct((8, width), f32),
        ],
        [
            pltpu.VMEM((size, 2 * length, 2 * width), f32),
            pltpu.VMEM((size, 2 * length, width), f32),
        ],
        flops=first_flops,
    )(*first_arrived, both, back_high, back_low)
    all_squares = [
        squares if k == 0 else lax.ppermute(squares, "chan", [(i, i ^ k) for i in range(columns)])
        for k in range(columns)
    ]
    input_codes, input_tails = run(
        functools.partial(second_kernel, order, length, second_places),
        "input_gradient", vmem_bytes,
        [
            jax.ShapeDtypeStruct((size, length, width), bf16),
            jax.ShapeDtypeStruct((size, tail_rows, width), f32),
        ],
        [
            pltpu.VMEM((size, 2 * length, width), f32),
            pltpu.VMEM((size, 2 * length, width), f32),
        ],
        flops=second_flops,
    )(*second_arrived, both, back_high, back_low, pair_spec)
    messages = run(
        functools.partial(message_kernel, size, length, columns),
        "messages", vmem_bytes,
        [jax.ShapeDtypeStruct((2 * length + tail_rows, width), bf16)] * size,
    )(codes, tails, input_codes, input_tails, *all_squares)
    messages = {k: send(message, k) if k else message for k, message in zip(order, messages)}
    turns = chips[: far // 2] + chips[far:-1] + chips[far // 2 : far] + [0]
    turns = [k for chip in turns for k in (2 * chip, 2 * chip + 1)]

    clip_limit = 0.25 * math.sqrt(length * size * chan_width * columns)
    whole = size * width
    grad_rows, gain = out_grad, skip_gain[None, :]
    if width != part:
        spread = lambda a: jnp.pad(
            a.reshape(a.shape[0], size, part), ((0, 0), (0, 0), (0, width - part))
        ).reshape(a.shape[0], whole)
        grad_rows, gain = spread(grad_rows), spread(gain)
    input_grad, filter_grad, skip_grad = run(
        functools.partial(last_kernel, turns, length, width, clip_limit),
        "outputs", vmem_bytes,
        [
            jax.ShapeDtypeStruct((length, whole), f32),
            jax.ShapeDtypeStruct((length, whole), f32),
            jax.ShapeDtypeStruct((1, whole), f32),
        ],
    )(*[messages[k] for k in turns], grad_rows, gain)
    if width != part:
        gather = lambda a: a.reshape(a.shape[0], size, width)[:, :, :part].reshape(
            a.shape[0], chan_width
        )
        input_grad, filter_grad, skip_grad = gather(input_grad), gather(filter_grad), gather(skip_grad)
    return (input_grad, filter_grad, skip_grad[0])


def solution(mesh):
    return jax.shard_map(
        per_device,
        mesh=mesh,
        in_specs=(P("ctx", "chan"), P("ctx", "chan"), P("ctx", "chan"), P("chan")),
        out_specs=(P("ctx", "chan"), P("ctx", "chan"), P("chan")),
        check_vma=False,
    )
```

```python
import functools
import math

import jax
import jax.numpy as jnp
import numpy as np
from jax import lax
from jax.experimental import pallas as pl
from jax.experimental.pallas import tpu as pltpu
from jax.sharding import PartitionSpec as P

epsilon = 1e-06
octaves = 246
low_power = 120
top_code = 128 * octaves - 1
tail_rows = 16
first_flops = 4 * 10**9
second_flops = 2 * 10**10


def tables(length):
    odd = 2 * np.arange(length) + 1
    phase = odd[:, None] * np.arange(length)[None, :] % (4 * length)
    angles = np.pi * phase / (2 * length)
    forward = np.concatenate([np.cos(angles), -np.sin(angles)], axis=0)
    high = forward.astype(np.float32).astype(jnp.bfloat16)
    low = (forward - high.astype(np.float64)).astype(np.float32).astype(jnp.bfloat16)
    both = np.concatenate([high, low], axis=1)
    scale = np.float32(1.0 / length)
    back_high = (high.astype(np.float32).T * scale).astype(jnp.bfloat16)
    back_low = (low.astype(np.float32).T * scale).astype(jnp.bfloat16)
    return jnp.asarray(both), jnp.asarray(back_high), jnp.asarray(back_low)


def three_parts(value):
    high = value.astype(jnp.bfloat16).astype(jnp.float32)
    rest = value - high
    middle = rest.astype(jnp.bfloat16).astype(jnp.float32)
    return high, middle, rest - middle


def encode(values):
    peak = jnp.max(jnp.abs(values), axis=0, keepdims=True) * (1.0 + 2.0**-7)
    scale = jnp.maximum(peak.astype(jnp.bfloat16).astype(jnp.float32), 2.0**-110)
    size = jnp.abs(values) * (top_code / 128.0 / scale)
    octave = jnp.floor(size)
    carrier = (size - octave + 1.0) * jnp.exp2(octave - float(low_power))
    return jnp.where(values < 0, -carrier, carrier).astype(jnp.bfloat16), scale


def decode(codes, scale):
    carrier = codes.astype(jnp.float32)
    size = jnp.abs(carrier)
    power = jnp.floor(jnp.log2(size) + 0.001)
    octaves_up = size * jnp.exp2(-power) + (power + float(low_power - 1))
    scale *= 128.0 / top_code
    return octaves_up * jnp.where(carrier < 0, -scale, scale)


def tail_tile(first_row, rows, width):
    row_ids = lax.broadcasted_iota(jnp.int32, (tail_rows, width), 0)
    tile = jnp.zeros((tail_rows, width), jnp.float32)
    for i, row in enumerate(rows):
        tile = jnp.where(
            row_ids == first_row + i, jnp.broadcast_to(row, (tail_rows, width)), tile
        )
    return tile


def correlate_rows(pairs, others, size):
    sums = [real + imag for real, imag in pairs]
    turned = [(real, real - imag, real + imag) for real, imag in others]
    results = []
    for p in range(size):
        shared = first = second = None
        for q in range(p, size):
            real, less, more = turned[q - p]
            terms = sums[q] * real, pairs[q][1] * less, pairs[q][0] * more
            if q > p:
                terms = shared + terms[0], first + terms[1], second + terms[2]
            shared, first, second = terms
        results.append((shared - first, shared - second))
    return results


def send_results(position, order, acc, back_high, back_low, emit):
    width = acc.shape[2]
    for i in range(0, len(order), 2):
        spec = jnp.concatenate([acc[position ^ order[i]], acc[position ^ order[i + 1]]], axis=1)
        high = spec.astype(jnp.bfloat16)
        low = (spec - high.astype(jnp.float32)).astype(jnp.bfloat16)
        dot = functools.partial(jnp.dot, preferred_element_type=jnp.float32)
        block = dot(back_high[...], high) + dot(back_high[...], low) + dot(back_low[...], high)
        emit(i, block[:, :width])
        emit(i + 1, block[:, width:])


def columns_kernel(chips, direct, length, part, arrays, *refs):
    blocks, rest = refs[:-2], refs[-2:]
    position = lax.axis_index("ctx")

    def put(out, row, j, k):
        columns = pl.ds(pl.multiple_of((position ^ k) * part, part), part)
        out[row : row + length] = arrays[j, :, columns]

    for core in range(2):
        row = 0
        for i, chip in enumerate(chips):
            for j in range(3):
                if i < direct and j < 2:
                    put(blocks[2 * i + core], j * length, j, 2 * chip + core)
                else:
                    put(rest[core], row, j, 2 * chip + core)
                    row += length


def taps_kernel(rows, length, mine, sibling, *refs):
    tables, messages, held = refs[:3], refs[3:-3], refs[-3:]
    for table, place in zip(tables, held):
        place[...] = table[...]
    for row, message in zip(rows, messages):
        message[:length] = mine[row : row + length]
        message[length:] = sibling[row : row + length]


def first_kernel(order, length, places, *refs):
    size = len(order)
    both, back_high, back_low, codes_out, tails_out, pair_spec, squares, spec, acc = refs[-9:]
    width = spec.shape[2] // 2
    position = lax.axis_index("ctx")

    skip = jnp.zeros((1, width), jnp.float32)
    for i, k in enumerate(order):
        ref, row = places[i]
        grad, other = refs[ref][row : row + length], refs[ref][row + length : row + 2 * length]
        skip += jnp.sum(grad.astype(jnp.float32) * other.astype(jnp.float32), axis=0, keepdims=True)
        lanes = jnp.concatenate([grad, other], axis=1)
        spec[position ^ k] = jnp.dot(
            both[...], jnp.concatenate([lanes, lanes], axis=0), preferred_element_type=jnp.float32
        )

    flip = jnp.where(lax.broadcasted_iota(jnp.int32, (8, width), 0) % 2 == 0, 1.0, -1.0)

    def rows(r, carry):
        real_rows = pl.ds(pl.multiple_of(r * 8, 8), 8)
        imag_rows = pl.ds(pl.multiple_of(length + r * 8, 8), 8)
        grad = [(spec[q, real_rows, :width], spec[q, imag_rows, :width]) for q in range(size)]
        pairs = []
        for q in range(size):
            if q + 1 < size:
                real = grad[q][0] + flip * grad[q + 1][1]
                imag = grad[q][1] - flip * grad[q + 1][0]
            else:
                real, imag = grad[q]
            pair_spec[q, real_rows, :] = real
            pair_spec[q, imag_rows, :] = imag
            pairs.append((real, imag))
        others = [(spec[q, real_rows, width:], spec[q, imag_rows, width:]) for q in range(size)]
        for p, (real, imag) in enumerate(correlate_rows(pairs, others, size)):
            acc[p, real_rows, :] = real
            acc[p, imag_rows, :] = imag
        return carry

    lax.fori_loop(0, length // 8, rows, 0)
    skip_parts = three_parts(skip)
    squares[...] = jnp.zeros_like(squares)

    def emit(i, block):
        squares[...] += jnp.sum((block * block).reshape(length // 8, 8, width), axis=0)
        codes_out[i], scale = encode(block)
        tails_out[i] = tail_tile(0, (scale,) + skip_parts, width)

    send_results(position, order, acc, back_high, back_low, emit)


def second_kernel(order, length, places, *refs):
    size = len(order)
    both, back_high, back_low, pair_spec, codes_out, tails_out, spec, acc = refs[-8:]
    width = spec.shape[2]
    position = lax.axis_index("ctx")

    for i in range(0, size, 2):
        lanes = jnp.concatenate(
            [refs[ref][row : row + length] for ref, row in places[i : i + 2]], axis=1
        )
        both_specs = jnp.dot(
            both[...], jnp.concatenate([lanes, lanes], axis=0), preferred_element_type=jnp.float32
        )
        spec[position ^ order[i]] = both_specs[:, :width]
        spec[position ^ order[i + 1]] = both_specs[:, width:]

    def rows(r, carry):
        real_rows = pl.ds(pl.multiple_of(r * 8, 8), 8)
        imag_rows = pl.ds(pl.multiple_of(length + r * 8, 8), 8)
        pairs = [(pair_spec[q, real_rows, :], pair_spec[q, imag_rows, :]) for q in range(size)]
        others = [(spec[q, real_rows, :], spec[q, imag_rows, :]) for q in range(size)]
        for p, (real, imag) in enumerate(correlate_rows(pairs, others, size)):
            acc[p, real_rows, :] = real
            acc[p, imag_rows, :] = imag
        return carry

    lax.fori_loop(0, length // 8, rows, 0)

    def emit(i, block):
        codes_out[i], scale = encode(block)
        tails_out[i] = tail_tile(4, (scale,), width)

    send_results(position, order, acc, back_high, back_low, emit)


def message_kernel(size, length, sums, *refs):
    filter_codes, filter_tails, input_codes, input_tails = refs[:4]
    partial_squares, out = refs[4 : 4 + sums], refs[4 + sums :]
    squares = partial_squares[0][...]
    for other in partial_squares[1:]:
        squares += other[...]
    total = jnp.sum(jnp.sum(squares, axis=0, keepdims=True), axis=1, keepdims=True)
    width = squares.shape[1]
    total_rows = tail_tile(5, three_parts(jnp.broadcast_to(total, (1, width))), width)
    for i in range(size):
        out[i][:length] = filter_codes[i]
        out[i][length : 2 * length] = input_codes[i]
        tail = filter_tails[i] + input_tails[i] + total_rows
        out[i][2 * length :] = tail.astype(jnp.bfloat16)


def last_kernel(order, length, part, clip_limit, *refs):
    size = len(order)
    messages = refs[:size]
    grad, gain, input_grad, filter_grad, skip_grad = refs[size:]
    position = lax.axis_index("ctx")
    total = jnp.zeros((1, part), jnp.float32)
    for message in messages:
        tail = message[2 * length :].astype(jnp.float32)
        total += tail[5:6] + tail[6:7] + tail[7:8]
    factor = jnp.minimum(1.0, clip_limit / jnp.sqrt(total + epsilon))
    for k, message in zip(order, messages):
        columns = pl.ds(pl.multiple_of((position ^ k) * part, part), part)
        tail = message[2 * length :].astype(jnp.float32)
        filter_grad[:, columns] = decode(message[:length], tail[0:1]) * factor
        skip_grad[:, columns] = tail[1:2] + tail[2:3] + tail[3:4]
        input_grad[:, columns] = (
            decode(message[length : 2 * length], tail[4:5])
            + gain[:, columns] * grad[:, columns].astype(jnp.float32)
        )


def run(kernel, name, vmem_bytes, out_shape, scratch=(), flops=10**9, **specs):
    return pl.pallas_call(
        kernel,
        out_shape=out_shape,
        scratch_shapes=scratch,
        name=name,
        **specs,
        cost_estimate=pl.CostEstimate(flops=flops, bytes_accessed=0, transcendentals=0),
        compiler_params=pltpu.CompilerParams(vmem_limit_bytes=vmem_bytes),
    )


def per_device(inputs, filter_taps, out_grad, skip_gain):
    length, chan_width = inputs.shape
    size = lax.axis_size("ctx")
    columns = lax.axis_size("chan")
    part = chan_width // size
    width = -(-part // 128) * 128
    position = lax.axis_index("ctx")
    both, back_high, back_low = tables(length)
    f32, bf16 = jnp.float32, jnp.bfloat16
    chips = sorted(range(size // 2), key=lambda chip: (-chip.bit_length(), -chip))
    order = [k for chip in chips for k in (2 * chip, 2 * chip + 1)]
    far = size // 4
    vmem_bytes = (8 + size) * 2**20

    def columns_for(array, k):
        block = lax.dynamic_slice_in_dim(array, (position ^ k) * part, part, 1)
        return jnp.pad(block, ((0, 0), (0, width - part)))

    def send(block, k):
        return lax.ppermute(block, "ctx", [(i, i ^ k) for i in range(size)])

    three = (out_grad, inputs, filter_taps)
    direct = size // 8
    rest_rows = (3 * len(chips) - 2 * direct) * length
    if width == part:
        *blocks, mine, others = run(
            functools.partial(columns_kernel, chips, direct, length, part),
            "columns", vmem_bytes,
            [jax.ShapeDtypeStruct((2 * length, width), bf16)] * (2 * direct)
            + [jax.ShapeDtypeStruct((rest_rows, width), bf16)] * 2,
        )(jnp.stack(three))
    else:
        blocks = [jnp.concatenate([columns_for(a, k) for a in three[:2]]) for k in order[: 2 * direct]]
        mine, others = (
            jnp.concatenate(
                [
                    columns_for(a, 2 * chip + core)
                    for i, chip in enumerate(chips)
                    for a in (three[2:] if i < direct else three)
                ]
            )
            for core in range(2)
        )

    sibling = send(others, 1)
    arrived = [send(block, k) for k, block in zip(order, blocks)]
    first_places = [(i, 0) for i in range(2 * direct)]
    taps_rows = [i * length for i in range(direct)]
    row = direct * length
    near_places = []
    for i, chip in enumerate(chips[direct:-1]):
        here = len(arrived)
        rows = (2 if i < far - direct else 3) * length
        pair = jnp.concatenate([held[row : row + rows] for held in (mine, sibling)])
        first_places += [(here, 0), (here, rows)]
        arrived.append(send(pair, 2 * chip))
        if i < far - direct:
            taps_rows.append(row + 2 * length)
        else:
            near_places += [(here, 2 * length), (here, 5 * length)]
        row += 3 * length
    first_places += [(len(arrived), row), (len(arrived) + 1, row)]
    first_arrived = [*arrived, mine, sibling]
    later = lax.optimization_barrier((mine, sibling, *arrived[: 2 * direct]))[:2]
    *tap_messages, both, back_high, back_low = run(
        functools.partial(taps_kernel, taps_rows, length),
        "taps", vmem_bytes,
        [jax.ShapeDtypeStruct((2 * length, width), bf16)] * len(taps_rows)
        + [jax.ShapeDtypeStruct(t.shape, t.dtype) for t in (both, back_high, back_low)],
    )(*later, both, back_high, back_low)
    arrived_taps = [send(block, 2 * chip) for chip, block in zip(chips, tap_messages)]
    second_places = [(i, half) for i in range(far) for half in (0, length)]
    second_places += [(ref - 2 * direct - (far - direct) + far, at) for ref, at in near_places]
    second_arrived = [*arrived_taps, *arrived[direct + far :], mine, sibling]
    second_places += [(len(second_arrived) - 2 + i, row + 2 * length) for i in range(2)]

    codes, tails, pair_spec, squares = run(
        functools.partial(first_kernel, order, length, first_places),
        "filter_gradient", vmem_bytes,
        [
            jax.ShapeDtypeStruct((size, length, width), bf16),
            jax.ShapeDtypeStruct((size, tail_rows, width), f32),
            jax.ShapeDtypeStruct((size, 2 * length, width), f32),
            jax.ShapeDtypeStruct((8, width), f32),
        ],
        [
            pltpu.VMEM((size, 2 * length, 2 * width), f32),
            pltpu.VMEM((size, 2 * length, width), f32),
        ],
        flops=first_flops,
    )(*first_arrived, both, back_high, back_low)
    all_squares = [
        squares if k == 0 else lax.ppermute(squares, "chan", [(i, i ^ k) for i in range(columns)])
        for k in range(columns)
    ]
    input_codes, input_tails = run(
        functools.partial(second_kernel, order, length, second_places),
        "input_gradient", vmem_bytes,
        [
            jax.ShapeDtypeStruct((size, length, width), bf16),
            jax.ShapeDtypeStruct((size, tail_rows, width), f32),
        ],
        [
            pltpu.VMEM((size, 2 * length, width), f32),
            pltpu.VMEM((size, 2 * length, width), f32),
        ],
        flops=second_flops,
    )(*second_arrived, both, back_high, back_low, pair_spec)
    messages = run(
        functools.partial(message_kernel, size, length, columns),
        "messages", vmem_bytes,
        [jax.ShapeDtypeStruct((2 * length + tail_rows, width), bf16)] * size,
    )(codes, tails, input_codes, input_tails, *all_squares)
    messages = {k: send(message, k) if k else message for k, message in zip(order, messages)}
    nearer = sorted(chips[:far])
    turns = nearer[: far // 2] + chips[far:-1] + nearer[far // 2 :] + [0]
    turns = [k for chip in turns for k in (2 * chip, 2 * chip + 1)]

    clip_limit = 0.25 * math.sqrt(length * size * chan_width * columns)
    whole = size * width
    grad_rows, gain = out_grad, skip_gain[None, :]
    if width != part:
        spread = lambda a: jnp.pad(
            a.reshape(a.shape[0], size, part), ((0, 0), (0, 0), (0, width - part))
        ).reshape(a.shape[0], whole)
        grad_rows, gain = spread(grad_rows), spread(gain)
    input_grad, filter_grad, skip_grad = run(
        functools.partial(last_kernel, turns, length, width, clip_limit),
        "outputs", vmem_bytes,
        [
            jax.ShapeDtypeStruct((length, whole), f32),
            jax.ShapeDtypeStruct((length, whole), f32),
            jax.ShapeDtypeStruct((1, whole), f32),
        ],
    )(*[messages[k] for k in turns], grad_rows, gain)
    if width != part:
        gather = lambda a: a.reshape(a.shape[0], size, width)[:, :, :part].reshape(
            a.shape[0], chan_width
        )
        input_grad, filter_grad, skip_grad = gather(input_grad), gather(filter_grad), gather(skip_grad)
    return (input_grad, filter_grad, skip_grad[0])


def solution(mesh):
    return jax.shard_map(
        per_device,
        mesh=mesh,
        in_specs=(P("ctx", "chan"), P("ctx", "chan"), P("ctx", "chan"), P("chan")),
        out_specs=(P("ctx", "chan"), P("ctx", "chan"), P("chan")),
        check_vma=False,
    )
```

```python
import functools
import math

import jax
import jax.numpy as jnp
import numpy as np
from jax import lax
from jax.experimental import pallas as pl
from jax.experimental.pallas import tpu as pltpu
from jax.sharding import PartitionSpec as P

epsilon = 1e-06
octaves = 246
low_power = 120
top_code = 128 * octaves - 1
tail_rows = 16
first_flops = 4 * 10**9
second_flops = 2 * 10**10


def tables(length):
    odd = 2 * np.arange(length) + 1
    phase = odd[:, None] * np.arange(length)[None, :] % (4 * length)
    angles = np.pi * phase / (2 * length)
    forward = np.concatenate([np.cos(angles), -np.sin(angles)], axis=0)
    high = forward.astype(np.float32).astype(jnp.bfloat16)
    low = (forward - high.astype(np.float64)).astype(np.float32).astype(jnp.bfloat16)
    both = np.concatenate([high, low], axis=1)
    scale = np.float32(1.0 / length)
    back_high = (high.astype(np.float32).T * scale).astype(jnp.bfloat16)
    back_low = (low.astype(np.float32).T * scale).astype(jnp.bfloat16)
    return jnp.asarray(both), jnp.asarray(back_high), jnp.asarray(back_low)


def three_parts(value):
    high = value.astype(jnp.bfloat16).astype(jnp.float32)
    rest = value - high
    middle = rest.astype(jnp.bfloat16).astype(jnp.float32)
    return high, middle, rest - middle


def encode(values):
    peak = jnp.max(jnp.abs(values), axis=0, keepdims=True) * (1.0 + 2.0**-7)
    scale = jnp.maximum(peak.astype(jnp.bfloat16).astype(jnp.float32), 2.0**-110)
    size = jnp.abs(values) * (top_code / 128.0 / scale)
    octave = jnp.floor(size)
    carrier = (size - octave + 1.0) * jnp.exp2(octave - float(low_power))
    return jnp.where(values < 0, -carrier, carrier).astype(jnp.bfloat16), scale


def decode(codes, scale):
    carrier = codes.astype(jnp.float32)
    size = jnp.abs(carrier)
    power = jnp.floor(jnp.log2(size) + 0.001)
    octaves_up = size * jnp.exp2(-power) + (power + float(low_power - 1))
    scale *= 128.0 / top_code
    return octaves_up * jnp.where(carrier < 0, -scale, scale)


def tail_tile(first_row, rows, width):
    row_ids = lax.broadcasted_iota(jnp.int32, (tail_rows, width), 0)
    tile = jnp.zeros((tail_rows, width), jnp.float32)
    for i, row in enumerate(rows):
        tile = jnp.where(
            row_ids == first_row + i, jnp.broadcast_to(row, (tail_rows, width)), tile
        )
    return tile


def correlate_rows(pairs, others, size):
    sums = [real + imag for real, imag in pairs]
    turned = [(real, real - imag, real + imag) for real, imag in others]
    results = []
    for p in range(size):
        shared = first = second = None
        for q in range(p, size):
            real, less, more = turned[q - p]
            terms = sums[q] * real, pairs[q][1] * less, pairs[q][0] * more
            if q > p:
                terms = shared + terms[0], first + terms[1], second + terms[2]
            shared, first, second = terms
        results.append((shared - first, shared - second))
    return results


def send_results(position, order, acc, back_high, back_low, emit):
    width = acc.shape[2]
    for i in range(0, len(order), 2):
        spec = jnp.concatenate([acc[position ^ order[i]], acc[position ^ order[i + 1]]], axis=1)
        high = spec.astype(jnp.bfloat16)
        low = (spec - high.astype(jnp.float32)).astype(jnp.bfloat16)
        dot = functools.partial(jnp.dot, preferred_element_type=jnp.float32)
        block = dot(back_high[...], high) + dot(back_high[...], low) + dot(back_low[...], high)
        emit(i, block[:, :width])
        emit(i + 1, block[:, width:])


def columns_kernel(chips, direct, length, part, arrays, *refs):
    blocks, rest = refs[:-2], refs[-2:]
    position = lax.axis_index("ctx")

    def put(out, row, j, k):
        columns = pl.ds(pl.multiple_of((position ^ k) * part, part), part)
        out[row : row + length] = arrays[j, :, columns]

    for core in range(2):
        row = 0
        for i, chip in enumerate(chips):
            for j in range(3):
                if i < direct and j < 2:
                    put(blocks[2 * i + core], j * length, j, 2 * chip + core)
                else:
                    put(rest[core], row, j, 2 * chip + core)
                    row += length


def taps_kernel(rows, length, mine, sibling, *refs):
    tables, messages, held = refs[:3], refs[3:-3], refs[-3:]
    for table, place in zip(tables, held):
        place[...] = table[...]
    for row, message in zip(rows, messages):
        message[:length] = mine[row : row + length]
        message[length:] = sibling[row : row + length]


def first_kernel(order, length, places, *refs):
    size = len(order)
    both, back_high, back_low, blocks_out, skip_out, pair_spec, squares, spec, acc = refs[-9:]
    width = spec.shape[2] // 2
    position = lax.axis_index("ctx")

    skip = jnp.zeros((1, width), jnp.float32)
    for i, k in enumerate(order):
        ref, row = places[i]
        grad, other = refs[ref][row : row + length], refs[ref][row + length : row + 2 * length]
        skip += jnp.sum(grad.astype(jnp.float32) * other.astype(jnp.float32), axis=0, keepdims=True)
        lanes = jnp.concatenate([grad, other], axis=1)
        spec[position ^ k] = jnp.dot(
            both[...], jnp.concatenate([lanes, lanes], axis=0), preferred_element_type=jnp.float32
        )

    flip = jnp.where(lax.broadcasted_iota(jnp.int32, (8, width), 0) % 2 == 0, 1.0, -1.0)

    def rows(r, carry):
        real_rows = pl.ds(pl.multiple_of(r * 8, 8), 8)
        imag_rows = pl.ds(pl.multiple_of(length + r * 8, 8), 8)
        grad = [(spec[q, real_rows, :width], spec[q, imag_rows, :width]) for q in range(size)]
        pairs = []
        for q in range(size):
            if q + 1 < size:
                real = grad[q][0] + flip * grad[q + 1][1]
                imag = grad[q][1] - flip * grad[q + 1][0]
            else:
                real, imag = grad[q]
            pair_spec[q, real_rows, :] = real
            pair_spec[q, imag_rows, :] = imag
            pairs.append((real, imag))
        others = [(spec[q, real_rows, width:], spec[q, imag_rows, width:]) for q in range(size)]
        for p, (real, imag) in enumerate(correlate_rows(pairs, others, size)):
            acc[p, real_rows, :] = real
            acc[p, imag_rows, :] = imag
        return carry

    lax.fori_loop(0, length // 8, rows, 0)
    skip_out[...] = skip
    squares[...] = jnp.zeros_like(squares)

    def emit(i, block):
        squares[...] += jnp.sum((block * block).reshape(length // 8, 8, width), axis=0)
        blocks_out[i] = block

    send_results(position, order, acc, back_high, back_low, emit)


def second_kernel(order, length, places, *refs):
    size = len(order)
    both, back_high, back_low, pair_spec, blocks, skip = refs[-12:-6]
    filter_codes, filter_tails, input_codes, input_tails, spec, acc = refs[-6:]
    width = spec.shape[2]
    position = lax.axis_index("ctx")

    for i in range(0, size, 2):
        lanes = jnp.concatenate(
            [refs[ref][row : row + length] for ref, row in places[i : i + 2]], axis=1
        )
        both_specs = jnp.dot(
            both[...], jnp.concatenate([lanes, lanes], axis=0), preferred_element_type=jnp.float32
        )
        spec[position ^ order[i]] = both_specs[:, :width]
        spec[position ^ order[i + 1]] = both_specs[:, width:]

    def rows(r, carry):
        real_rows = pl.ds(pl.multiple_of(r * 8, 8), 8)
        imag_rows = pl.ds(pl.multiple_of(length + r * 8, 8), 8)
        pairs = [(pair_spec[q, real_rows, :], pair_spec[q, imag_rows, :]) for q in range(size)]
        others = [(spec[q, real_rows, :], spec[q, imag_rows, :]) for q in range(size)]
        for p, (real, imag) in enumerate(correlate_rows(pairs, others, size)):
            acc[p, real_rows, :] = real
            acc[p, imag_rows, :] = imag
        return carry

    lax.fori_loop(0, length // 8, rows, 0)

    skip_parts = three_parts(skip[...])
    for i in range(size):
        filter_codes[i], scale = encode(blocks[i])
        filter_tails[i] = tail_tile(0, (scale,) + skip_parts, width)

    def emit(i, block):
        input_codes[i], scale = encode(block)
        input_tails[i] = tail_tile(4, (scale,), width)

    send_results(position, order, acc, back_high, back_low, emit)


def message_kernel(size, length, sums, *refs):
    filter_codes, filter_tails, input_codes, input_tails = refs[:4]
    partial_squares, out = refs[4 : 4 + sums], refs[4 + sums :]
    squares = partial_squares[0][...]
    for other in partial_squares[1:]:
        squares += other[...]
    total = jnp.sum(jnp.sum(squares, axis=0, keepdims=True), axis=1, keepdims=True)
    width = squares.shape[1]
    total_rows = tail_tile(5, three_parts(jnp.broadcast_to(total, (1, width))), width)
    for i in range(size):
        out[i][:length] = filter_codes[i]
        out[i][length : 2 * length] = input_codes[i]
        tail = filter_tails[i] + input_tails[i] + total_rows
        out[i][2 * length :] = tail.astype(jnp.bfloat16)


def last_kernel(order, length, part, clip_limit, *refs):
    size = len(order)
    messages = refs[:size]
    grad, gain, input_grad, filter_grad, skip_grad = refs[size:]
    position = lax.axis_index("ctx")
    total = jnp.zeros((1, part), jnp.float32)
    for message in messages:
        tail = message[2 * length :].astype(jnp.float32)
        total += tail[5:6] + tail[6:7] + tail[7:8]
    factor = jnp.minimum(1.0, clip_limit / jnp.sqrt(total + epsilon))
    for k, message in zip(order, messages):
        columns = pl.ds(pl.multiple_of((position ^ k) * part, part), part)
        tail = message[2 * length :].astype(jnp.float32)
        filter_grad[:, columns] = decode(message[:length], tail[0:1]) * factor
        skip_grad[:, columns] = tail[1:2] + tail[2:3] + tail[3:4]
        input_grad[:, columns] = (
            decode(message[length : 2 * length], tail[4:5])
            + gain[:, columns] * grad[:, columns].astype(jnp.float32)
        )


def run(kernel, name, vmem_bytes, out_shape, scratch=(), flops=10**9, **specs):
    return pl.pallas_call(
        kernel,
        out_shape=out_shape,
        scratch_shapes=scratch,
        name=name,
        **specs,
        cost_estimate=pl.CostEstimate(flops=flops, bytes_accessed=0, transcendentals=0),
        compiler_params=pltpu.CompilerParams(vmem_limit_bytes=vmem_bytes),
    )


def per_device(inputs, filter_taps, out_grad, skip_gain):
    length, chan_width = inputs.shape
    size = lax.axis_size("ctx")
    columns = lax.axis_size("chan")
    part = chan_width // size
    width = -(-part // 128) * 128
    position = lax.axis_index("ctx")
    both, back_high, back_low = tables(length)
    f32, bf16 = jnp.float32, jnp.bfloat16
    chips = sorted(range(size // 2), key=lambda chip: (-chip.bit_length(), -chip))
    order = [k for chip in chips for k in (2 * chip, 2 * chip + 1)]
    far = size // 4
    vmem_bytes = (8 + size) * 2**20

    def columns_for(array, k):
        block = lax.dynamic_slice_in_dim(array, (position ^ k) * part, part, 1)
        return jnp.pad(block, ((0, 0), (0, width - part)))

    def send(block, k):
        return lax.ppermute(block, "ctx", [(i, i ^ k) for i in range(size)])

    three = (out_grad, inputs, filter_taps)
    direct = size // 8
    rest_rows = (3 * len(chips) - 2 * direct) * length
    if width == part:
        *blocks, mine, others = run(
            functools.partial(columns_kernel, chips, direct, length, part),
            "columns", vmem_bytes,
            [jax.ShapeDtypeStruct((2 * length, width), bf16)] * (2 * direct)
            + [jax.ShapeDtypeStruct((rest_rows, width), bf16)] * 2,
        )(jnp.stack(three))
    else:
        blocks = [jnp.concatenate([columns_for(a, k) for a in three[:2]]) for k in order[: 2 * direct]]
        mine, others = (
            jnp.concatenate(
                [
                    columns_for(a, 2 * chip + core)
                    for i, chip in enumerate(chips)
                    for a in (three[2:] if i < direct else three)
                ]
            )
            for core in range(2)
        )

    sibling = send(others, 1)
    arrived = [send(block, k) for k, block in zip(order, blocks)]
    first_places = [(i, 0) for i in range(2 * direct)]
    taps_rows = [i * length for i in range(direct)]
    row = direct * length
    near_places = []
    for i, chip in enumerate(chips[direct:-1]):
        here = len(arrived)
        rows = (2 if i < far - direct else 3) * length
        pair = jnp.concatenate([held[row : row + rows] for held in (mine, sibling)])
        first_places += [(here, 0), (here, rows)]
        arrived.append(send(pair, 2 * chip))
        if i < far - direct:
            taps_rows.append(row + 2 * length)
        else:
            near_places += [(here, 2 * length), (here, 5 * length)]
        row += 3 * length
    first_places += [(len(arrived), row), (len(arrived) + 1, row)]
    first_arrived = [*arrived, mine, sibling]
    later = lax.optimization_barrier((mine, sibling, *arrived[: 2 * direct]))[:2]
    *tap_messages, both, back_high, back_low = run(
        functools.partial(taps_kernel, taps_rows, length),
        "taps", vmem_bytes,
        [jax.ShapeDtypeStruct((2 * length, width), bf16)] * len(taps_rows)
        + [jax.ShapeDtypeStruct(t.shape, t.dtype) for t in (both, back_high, back_low)],
    )(*later, both, back_high, back_low)
    arrived_taps = [send(block, 2 * chip) for chip, block in zip(chips, tap_messages)]
    second_places = [(i, half) for i in range(far) for half in (0, length)]
    second_places += [(ref - 2 * direct - (far - direct) + far, at) for ref, at in near_places]
    second_arrived = [*arrived_taps, *arrived[direct + far :], mine, sibling]
    second_places += [(len(second_arrived) - 2 + i, row + 2 * length) for i in range(2)]

    filter_blocks, skip, pair_spec, squares = run(
        functools.partial(first_kernel, order, length, first_places),
        "filter_gradient", vmem_bytes,
        [
            jax.ShapeDtypeStruct((size, length, width), f32),
            jax.ShapeDtypeStruct((1, width), f32),
            jax.ShapeDtypeStruct((size, 2 * length, width), f32),
            jax.ShapeDtypeStruct((8, width), f32),
        ],
        [
            pltpu.VMEM((size, 2 * length, 2 * width), f32),
            pltpu.VMEM((size, 2 * length, width), f32),
        ],
        flops=first_flops,
    )(*first_arrived, both, back_high, back_low)
    all_squares = [
        squares if k == 0 else lax.ppermute(squares, "chan", [(i, i ^ k) for i in range(columns)])
        for k in range(columns)
    ]
    codes_and_tails = run(
        functools.partial(second_kernel, order, length, second_places),
        "input_gradient", vmem_bytes,
        [
            jax.ShapeDtypeStruct((size, length, width), bf16),
            jax.ShapeDtypeStruct((size, tail_rows, width), f32),
        ]
        * 2,
        [
            pltpu.VMEM((size, 2 * length, width), f32),
            pltpu.VMEM((size, 2 * length, width), f32),
        ],
        flops=second_flops,
    )(*second_arrived, both, back_high, back_low, pair_spec, filter_blocks, skip)
    messages = run(
        functools.partial(message_kernel, size, length, columns),
        "messages", vmem_bytes,
        [jax.ShapeDtypeStruct((2 * length + tail_rows, width), bf16)] * size,
    )(*codes_and_tails, *all_squares)
    messages = {k: send(message, k) if k else message for k, message in zip(order, messages)}
    nearer = sorted(chips[:far])
    turns = nearer[: far // 2] + chips[far:-1] + nearer[far // 2 :] + [0]
    turns = [k for chip in turns for k in (2 * chip, 2 * chip + 1)]

    clip_limit = 0.25 * math.sqrt(length * size * chan_width * columns)
    whole = size * width
    grad_rows, gain = out_grad, skip_gain[None, :]
    if width != part:
        spread = lambda a: jnp.pad(
            a.reshape(a.shape[0], size, part), ((0, 0), (0, 0), (0, width - part))
        ).reshape(a.shape[0], whole)
        grad_rows, gain = spread(grad_rows), spread(gain)
    input_grad, filter_grad, skip_grad = run(
        functools.partial(last_kernel, turns, length, width, clip_limit),
        "outputs", vmem_bytes,
        [
            jax.ShapeDtypeStruct((length, whole), f32),
            jax.ShapeDtypeStruct((length, whole), f32),
            jax.ShapeDtypeStruct((1, whole), f32),
        ],
    )(*[messages[k] for k in turns], grad_rows, gain)
    if width != part:
        gather = lambda a: a.reshape(a.shape[0], size, width)[:, :, :part].reshape(
            a.shape[0], chan_width
        )
        input_grad, filter_grad, skip_grad = gather(input_grad), gather(filter_grad), gather(skip_grad)
    return (input_grad, filter_grad, skip_grad[0])


def solution(mesh):
    return jax.shard_map(
        per_device,
        mesh=mesh,
        in_specs=(P("ctx", "chan"), P("ctx", "chan"), P("ctx", "chan"), P("chan")),
        out_specs=(P("ctx", "chan"), P("ctx", "chan"), P("chan")),
        check_vma=False,
    )
```

```python
import functools
import math

import jax
import jax.numpy as jnp
import numpy as np
from jax import lax
from jax.experimental import pallas as pl
from jax.experimental.pallas import tpu as pltpu
from jax.sharding import PartitionSpec as P

epsilon = 1e-06
octaves = 246
low_power = 120
top_code = 128 * octaves - 1
tail_rows = 16
first_flops = 4 * 10**9
second_flops = 2 * 10**10


def tables(length):
    odd = 2 * np.arange(length) + 1
    phase = odd[:, None] * np.arange(length)[None, :] % (4 * length)
    angles = np.pi * phase / (2 * length)
    forward = np.concatenate([np.cos(angles), -np.sin(angles)], axis=0)
    high = forward.astype(np.float32).astype(jnp.bfloat16)
    low = (forward - high.astype(np.float64)).astype(np.float32).astype(jnp.bfloat16)
    both = np.concatenate([high, low], axis=1)
    scale = np.float32(1.0 / length)
    back_high = (high.astype(np.float32).T * scale).astype(jnp.bfloat16)
    back_low = (low.astype(np.float32).T * scale).astype(jnp.bfloat16)
    return jnp.asarray(both), jnp.asarray(back_high), jnp.asarray(back_low)


def three_parts(value):
    high = value.astype(jnp.bfloat16).astype(jnp.float32)
    rest = value - high
    middle = rest.astype(jnp.bfloat16).astype(jnp.float32)
    return high, middle, rest - middle


def encode(values):
    peak = jnp.max(jnp.abs(values), axis=0, keepdims=True) * (1.0 + 2.0**-7)
    scale = jnp.maximum(peak.astype(jnp.bfloat16).astype(jnp.float32), 2.0**-110)
    size = jnp.abs(values) * (top_code / 128.0 / scale)
    octave = jnp.floor(size)
    carrier = (size - octave + 1.0) * jnp.exp2(octave - float(low_power))
    return jnp.where(values < 0, -carrier, carrier).astype(jnp.bfloat16), scale


def decode(codes, scale):
    carrier = codes.astype(jnp.float32)
    size = jnp.abs(carrier)
    power = jnp.floor(jnp.log2(size) + 0.001)
    octaves_up = size * jnp.exp2(-power) + (power + float(low_power - 1))
    scale *= 128.0 / top_code
    return octaves_up * jnp.where(carrier < 0, -scale, scale)


def tail_tile(first_row, rows, width):
    row_ids = lax.broadcasted_iota(jnp.int32, (tail_rows, width), 0)
    tile = jnp.zeros((tail_rows, width), jnp.float32)
    for i, row in enumerate(rows):
        tile = jnp.where(
            row_ids == first_row + i, jnp.broadcast_to(row, (tail_rows, width)), tile
        )
    return tile


def correlate_rows(pairs, others, size):
    sums = [real + imag for real, imag in pairs]
    turned = [(real, real - imag, real + imag) for real, imag in others]
    results = []
    for p in range(size):
        shared = first = second = None
        for q in range(p, size):
            real, less, more = turned[q - p]
            terms = sums[q] * real, pairs[q][1] * less, pairs[q][0] * more
            if q > p:
                terms = shared + terms[0], first + terms[1], second + terms[2]
            shared, first, second = terms
        results.append((shared - first, shared - second))
    return results


def send_results(position, order, acc, back_high, back_low, emit):
    width = acc.shape[2]
    for i in range(0, len(order), 2):
        spec = jnp.concatenate([acc[position ^ order[i]], acc[position ^ order[i + 1]]], axis=1)
        high = spec.astype(jnp.bfloat16)
        low = (spec - high.astype(jnp.float32)).astype(jnp.bfloat16)
        dot = functools.partial(jnp.dot, preferred_element_type=jnp.float32)
        block = dot(back_high[...], high) + dot(back_high[...], low) + dot(back_low[...], high)
        emit(i, block[:, :width])
        emit(i + 1, block[:, width:])


def columns_kernel(chips, direct, length, part, arrays, *refs):
    blocks, rest = refs[:-2], refs[-2:]
    position = lax.axis_index("ctx")

    def put(out, row, j, k):
        columns = pl.ds(pl.multiple_of((position ^ k) * part, part), part)
        out[row : row + length] = arrays[j, :, columns]

    for core in range(2):
        row = 0
        for i, chip in enumerate(chips):
            for j in range(3):
                if i < direct and j < 2:
                    put(blocks[2 * i + core], j * length, j, 2 * chip + core)
                else:
                    put(rest[core], row, j, 2 * chip + core)
                    row += length


def taps_kernel(rows, length, mine, sibling, *refs):
    tables, messages, held = refs[:3], refs[3:-3], refs[-3:]
    for table, place in zip(tables, held):
        place[...] = table[...]
    for row, message in zip(rows, messages):
        message[:length] = mine[row : row + length]
        message[length:] = sibling[row : row + length]


def first_kernel(order, length, places, *refs):
    size = len(order)
    both, back_high, back_low, blocks_out, skip_out, pair_spec, squares, spec, acc = refs[-9:]
    width = spec.shape[2] // 2
    position = lax.axis_index("ctx")

    skip = jnp.zeros((1, width), jnp.float32)
    for i, k in enumerate(order):
        ref, row = places[i]
        grad, other = refs[ref][row : row + length], refs[ref][row + length : row + 2 * length]
        skip += jnp.sum(grad.astype(jnp.float32) * other.astype(jnp.float32), axis=0, keepdims=True)
        lanes = jnp.concatenate([grad, other], axis=1)
        spec[position ^ k] = jnp.dot(
            both[...], jnp.concatenate([lanes, lanes], axis=0), preferred_element_type=jnp.float32
        )

    flip = jnp.where(lax.broadcasted_iota(jnp.int32, (8, width), 0) % 2 == 0, 1.0, -1.0)

    def rows(r, carry):
        real_rows = pl.ds(pl.multiple_of(r * 8, 8), 8)
        imag_rows = pl.ds(pl.multiple_of(length + r * 8, 8), 8)
        grad = [(spec[q, real_rows, :width], spec[q, imag_rows, :width]) for q in range(size)]
        pairs = []
        for q in range(size):
            if q + 1 < size:
                real = grad[q][0] + flip * grad[q + 1][1]
                imag = grad[q][1] - flip * grad[q + 1][0]
            else:
                real, imag = grad[q]
            pair_spec[q, real_rows, :] = real
            pair_spec[q, imag_rows, :] = imag
            pairs.append((real, imag))
        others = [(spec[q, real_rows, width:], spec[q, imag_rows, width:]) for q in range(size)]
        for p, (real, imag) in enumerate(correlate_rows(pairs, others, size)):
            acc[p, real_rows, :] = real
            acc[p, imag_rows, :] = imag
        return carry

    lax.fori_loop(0, length // 8, rows, 0)
    skip_out[...] = skip
    squares[...] = jnp.zeros_like(squares)

    def emit(i, block):
        squares[...] += jnp.sum((block * block).reshape(length // 8, 8, width), axis=0)
        blocks_out[i] = block

    send_results(position, order, acc, back_high, back_low, emit)


def second_kernel(order, length, places, *refs):
    size = len(order)
    both, back_high, back_low, pair_spec, blocks, skip = refs[-12:-6]
    filter_codes, filter_tails, input_codes, input_tails, spec, acc = refs[-6:]
    width = spec.shape[2]
    position = lax.axis_index("ctx")

    for i in range(0, size, 2):
        lanes = jnp.concatenate(
            [refs[ref][row : row + length] for ref, row in places[i : i + 2]], axis=1
        )
        both_specs = jnp.dot(
            both[...], jnp.concatenate([lanes, lanes], axis=0), preferred_element_type=jnp.float32
        )
        spec[position ^ order[i]] = both_specs[:, :width]
        spec[position ^ order[i + 1]] = both_specs[:, width:]

    def rows(r, carry):
        real_rows = pl.ds(pl.multiple_of(r * 8, 8), 8)
        imag_rows = pl.ds(pl.multiple_of(length + r * 8, 8), 8)
        pairs = [(pair_spec[q, real_rows, :], pair_spec[q, imag_rows, :]) for q in range(size)]
        others = [(spec[q, real_rows, :], spec[q, imag_rows, :]) for q in range(size)]
        for p, (real, imag) in enumerate(correlate_rows(pairs, others, size)):
            acc[p, real_rows, :] = real
            acc[p, imag_rows, :] = imag
        return carry

    lax.fori_loop(0, length // 8, rows, 0)

    skip_parts = three_parts(skip[...])
    for i in range(size):
        filter_codes[i], scale = encode(blocks[i])
        filter_tails[i] = tail_tile(0, (scale,) + skip_parts, width)

    def emit(i, block):
        input_codes[i], scale = encode(block)
        input_tails[i] = tail_tile(4, (scale,), width)

    send_results(position, order, acc, back_high, back_low, emit)


def message_kernel(size, length, sums, *refs):
    filter_codes, filter_tails, input_codes, input_tails = refs[:4]
    partial_squares, out = refs[4 : 4 + sums], refs[4 + sums :]
    squares = partial_squares[0][...]
    for other in partial_squares[1:]:
        squares += other[...]
    total = jnp.sum(jnp.sum(squares, axis=0, keepdims=True), axis=1, keepdims=True)
    width = squares.shape[1]
    total_rows = tail_tile(5, three_parts(jnp.broadcast_to(total, (1, width))), width)
    for i in range(size):
        out[i][:length] = filter_codes[i]
        out[i][length : 2 * length] = input_codes[i]
        tail = filter_tails[i] + input_tails[i] + total_rows
        out[i][2 * length :] = tail.astype(jnp.bfloat16)


def early_kernel(order, length, part, *refs):
    messages, (grad, gain, input_blocks, filter_blocks) = refs[:-4], refs[-4:]
    position = lax.axis_index("ctx")
    for i, (k, message) in enumerate(zip(order, messages)):
        columns = pl.ds(pl.multiple_of((position ^ k) * part, part), part)
        tail = message[2 * length :].astype(jnp.float32)
        filter_blocks[i] = decode(message[:length], tail[0:1])
        input_blocks[i] = (
            decode(message[length : 2 * length], tail[4:5])
            + gain[:, columns] * grad[:, columns].astype(jnp.float32)
        )


def last_kernel(order, early, length, part, clip_limit, *refs):
    size = len(order)
    messages = refs[:size]
    input_blocks, filter_blocks, grad, gain, input_grad, filter_grad, skip_grad = refs[size:]
    position = lax.axis_index("ctx")
    total = jnp.zeros((1, part), jnp.float32)
    for message in messages:
        tail = message[2 * length :].astype(jnp.float32)
        total += tail[5:6] + tail[6:7] + tail[7:8]
    factor = jnp.minimum(1.0, clip_limit / jnp.sqrt(total + epsilon))
    for i, (k, message) in enumerate(zip(order, messages)):
        columns = pl.ds(pl.multiple_of((position ^ k) * part, part), part)
        tail = message[2 * length :].astype(jnp.float32)
        skip_grad[:, columns] = tail[1:2] + tail[2:3] + tail[3:4]
        if i < early:
            filter_grad[:, columns] = filter_blocks[i] * factor
            input_grad[:, columns] = input_blocks[i]
        else:
            filter_grad[:, columns] = decode(message[:length], tail[0:1]) * factor
            input_grad[:, columns] = (
                decode(message[length : 2 * length], tail[4:5])
                + gain[:, columns] * grad[:, columns].astype(jnp.float32)
            )


def run(kernel, name, vmem_bytes, out_shape, scratch=(), flops=10**9, **specs):
    return pl.pallas_call(
        kernel,
        out_shape=out_shape,
        scratch_shapes=scratch,
        name=name,
        **specs,
        cost_estimate=pl.CostEstimate(flops=flops, bytes_accessed=0, transcendentals=0),
        compiler_params=pltpu.CompilerParams(vmem_limit_bytes=vmem_bytes),
    )


def per_device(inputs, filter_taps, out_grad, skip_gain):
    length, chan_width = inputs.shape
    size = lax.axis_size("ctx")
    columns = lax.axis_size("chan")
    part = chan_width // size
    width = -(-part // 128) * 128
    position = lax.axis_index("ctx")
    both, back_high, back_low = tables(length)
    f32, bf16 = jnp.float32, jnp.bfloat16
    chips = sorted(range(size // 2), key=lambda chip: (-chip.bit_length(), -chip))
    order = [k for chip in chips for k in (2 * chip, 2 * chip + 1)]
    far = size // 4
    vmem_bytes = (8 + size) * 2**20

    def columns_for(array, k):
        block = lax.dynamic_slice_in_dim(array, (position ^ k) * part, part, 1)
        return jnp.pad(block, ((0, 0), (0, width - part)))

    def send(block, k):
        return lax.ppermute(block, "ctx", [(i, i ^ k) for i in range(size)])

    three = (out_grad, inputs, filter_taps)
    direct = size // 8
    rest_rows = (3 * len(chips) - 2 * direct) * length
    if width == part:
        *blocks, mine, others = run(
            functools.partial(columns_kernel, chips, direct, length, part),
            "columns", vmem_bytes,
            [jax.ShapeDtypeStruct((2 * length, width), bf16)] * (2 * direct)
            + [jax.ShapeDtypeStruct((rest_rows, width), bf16)] * 2,
        )(jnp.stack(three))
    else:
        blocks = [jnp.concatenate([columns_for(a, k) for a in three[:2]]) for k in order[: 2 * direct]]
        mine, others = (
            jnp.concatenate(
                [
                    columns_for(a, 2 * chip + core)
                    for i, chip in enumerate(chips)
                    for a in (three[2:] if i < direct else three)
                ]
            )
            for core in range(2)
        )

    sibling = send(others, 1)
    arrived = [send(block, k) for k, block in zip(order, blocks)]
    first_places = [(i, 0) for i in range(2 * direct)]
    taps_rows = [i * length for i in range(direct)]
    row = direct * length
    near_places = []
    for i, chip in enumerate(chips[direct:-1]):
        here = len(arrived)
        rows = (2 if i < far - direct else 3) * length
        pair = jnp.concatenate([held[row : row + rows] for held in (mine, sibling)])
        first_places += [(here, 0), (here, rows)]
        arrived.append(send(pair, 2 * chip))
        if i < far - direct:
            taps_rows.append(row + 2 * length)
        else:
            near_places += [(here, 2 * length), (here, 5 * length)]
        row += 3 * length
    first_places += [(len(arrived), row), (len(arrived) + 1, row)]
    first_arrived = [*arrived, mine, sibling]
    later = lax.optimization_barrier((mine, sibling, *arrived[: 2 * direct]))[:2]
    *tap_messages, both, back_high, back_low = run(
        functools.partial(taps_kernel, taps_rows, length),
        "taps", vmem_bytes,
        [jax.ShapeDtypeStruct((2 * length, width), bf16)] * len(taps_rows)
        + [jax.ShapeDtypeStruct(t.shape, t.dtype) for t in (both, back_high, back_low)],
    )(*later, both, back_high, back_low)
    arrived_taps = [send(block, 2 * chip) for chip, block in zip(chips, tap_messages)]
    second_places = [(i, half) for i in range(far) for half in (0, length)]
    second_places += [(ref - 2 * direct - (far - direct) + far, at) for ref, at in near_places]
    second_arrived = [*arrived_taps, *arrived[direct + far :], mine, sibling]
    second_places += [(len(second_arrived) - 2 + i, row + 2 * length) for i in range(2)]

    filter_blocks, skip, pair_spec, squares = run(
        functools.partial(first_kernel, order, length, first_places),
        "filter_gradient", vmem_bytes,
        [
            jax.ShapeDtypeStruct((size, length, width), f32),
            jax.ShapeDtypeStruct((1, width), f32),
            jax.ShapeDtypeStruct((size, 2 * length, width), f32),
            jax.ShapeDtypeStruct((8, width), f32),
        ],
        [
            pltpu.VMEM((size, 2 * length, 2 * width), f32),
            pltpu.VMEM((size, 2 * length, width), f32),
        ],
        flops=first_flops,
    )(*first_arrived, both, back_high, back_low)
    all_squares = [
        squares if k == 0 else lax.ppermute(squares, "chan", [(i, i ^ k) for i in range(columns)])
        for k in range(columns)
    ]
    codes_and_tails = run(
        functools.partial(second_kernel, order, length, second_places),
        "input_gradient", vmem_bytes,
        [
            jax.ShapeDtypeStruct((size, length, width), bf16),
            jax.ShapeDtypeStruct((size, tail_rows, width), f32),
        ]
        * 2,
        [
            pltpu.VMEM((size, 2 * length, width), f32),
            pltpu.VMEM((size, 2 * length, width), f32),
        ],
        flops=second_flops,
    )(*second_arrived, both, back_high, back_low, pair_spec, filter_blocks, skip)
    messages = run(
        functools.partial(message_kernel, size, length, columns),
        "messages", vmem_bytes,
        [jax.ShapeDtypeStruct((2 * length + tail_rows, width), bf16)] * size,
    )(*codes_and_tails, *all_squares)
    messages = {k: send(message, k) if k else message for k, message in zip(order, messages)}
    nearer = sorted(chips[:far])
    turns = nearer[: far // 2] + chips[far:-1] + nearer[far // 2 :] + [0]
    turns = [k for chip in turns for k in (2 * chip, 2 * chip + 1)]

    clip_limit = 0.25 * math.sqrt(length * size * chan_width * columns)
    whole = size * width
    grad_rows, gain = out_grad, skip_gain[None, :]
    if width != part:
        spread = lambda a: jnp.pad(
            a.reshape(a.shape[0], size, part), ((0, 0), (0, 0), (0, width - part))
        ).reshape(a.shape[0], whole)
        grad_rows, gain = spread(grad_rows), spread(gain)
    turns = turns[: size // 2] + [0] + [k for k in turns[size // 2 :] if k]
    early = size // 2 + 1
    decoded = run(
        functools.partial(early_kernel, turns[:early], length, width),
        "early", vmem_bytes,
        [jax.ShapeDtypeStruct((early, length, width), f32)] * 2,
        flops=first_flops,
    )(*[messages[k] for k in turns[:early]], grad_rows, gain)
    input_grad, filter_grad, skip_grad = run(
        functools.partial(last_kernel, turns, early, length, width, clip_limit),
        "outputs", vmem_bytes,
        [
            jax.ShapeDtypeStruct((length, whole), f32),
            jax.ShapeDtypeStruct((length, whole), f32),
            jax.ShapeDtypeStruct((1, whole), f32),
        ],
    )(*[messages[k] for k in turns], *decoded, grad_rows, gain)
    if width != part:
        gather = lambda a: a.reshape(a.shape[0], size, width)[:, :, :part].reshape(
            a.shape[0], chan_width
        )
        input_grad, filter_grad, skip_grad = gather(input_grad), gather(filter_grad), gather(skip_grad)
    return (input_grad, filter_grad, skip_grad[0])


def solution(mesh):
    return jax.shard_map(
        per_device,
        mesh=mesh,
        in_specs=(P("ctx", "chan"), P("ctx", "chan"), P("ctx", "chan"), P("chan")),
        out_specs=(P("ctx", "chan"), P("ctx", "chan"), P("chan")),
        check_vma=False,
    )
```

```python
import functools
import math

import jax
import jax.numpy as jnp
import numpy as np
from jax import lax
from jax.experimental import pallas as pl
from jax.experimental.pallas import tpu as pltpu
from jax.sharding import PartitionSpec as P

epsilon = 1e-06
octaves = 246
low_power = 120
top_code = 128 * octaves - 1
tail_rows = 16
first_flops = 4 * 10**9
second_flops = 2 * 10**10


def tables(length):
    odd = 2 * np.arange(length) + 1
    phase = odd[:, None] * np.arange(length)[None, :] % (4 * length)
    angles = np.pi * phase / (2 * length)
    forward = np.concatenate([np.cos(angles), -np.sin(angles)], axis=0)
    high = forward.astype(np.float32).astype(jnp.bfloat16)
    low = (forward - high.astype(np.float64)).astype(np.float32).astype(jnp.bfloat16)
    both = np.concatenate([high, low], axis=1)
    scale = np.float32(1.0 / length)
    back_high = (high.astype(np.float32).T * scale).astype(jnp.bfloat16)
    back_low = (low.astype(np.float32).T * scale).astype(jnp.bfloat16)
    return jnp.asarray(both), jnp.asarray(back_high), jnp.asarray(back_low)


def three_parts(value):
    high = value.astype(jnp.bfloat16).astype(jnp.float32)
    rest = value - high
    middle = rest.astype(jnp.bfloat16).astype(jnp.float32)
    return high, middle, rest - middle


def encode(values):
    peak = jnp.max(jnp.abs(values), axis=0, keepdims=True) * (1.0 + 2.0**-7)
    scale = jnp.maximum(peak.astype(jnp.bfloat16).astype(jnp.float32), 2.0**-116)
    size = jnp.abs(values) * (top_code / 128.0 / scale)
    octave = jnp.floor(size)
    carrier = (size - octave + 1.0) * jnp.exp2(octave - float(low_power))
    return jnp.where(values < 0, -carrier, carrier).astype(jnp.bfloat16), scale


def decode(codes, scale):
    carrier = codes.astype(jnp.float32)
    size = jnp.abs(carrier)
    power = jnp.floor(jnp.log2(size) + 0.001)
    octaves_up = size * jnp.exp2(-power) + (power + float(low_power - 1))
    scale *= 128.0 / top_code
    return octaves_up * jnp.where(carrier < 0, -scale, scale)


def tail_tile(first_row, rows, width):
    row_ids = lax.broadcasted_iota(jnp.int32, (tail_rows, width), 0)
    tile = jnp.zeros((tail_rows, width), jnp.float32)
    for i, row in enumerate(rows):
        tile = jnp.where(
            row_ids == first_row + i, jnp.broadcast_to(row, (tail_rows, width)), tile
        )
    return tile


def correlate_rows(pairs, others, size):
    sums = [real + imag for real, imag in pairs]
    turned = [(real, real - imag, real + imag) for real, imag in others]
    results = []
    for p in range(size):
        shared = first = second = None
        for q in range(p, size):
            real, less, more = turned[q - p]
            terms = sums[q] * real, pairs[q][1] * less, pairs[q][0] * more
            if q > p:
                terms = shared + terms[0], first + terms[1], second + terms[2]
            shared, first, second = terms
        results.append((shared - first, shared - second))
    return results


def send_results(position, order, acc, back_high, back_low, emit):
    width = acc.shape[2]
    for i in range(0, len(order), 2):
        spec = jnp.concatenate([acc[position ^ order[i]], acc[position ^ order[i + 1]]], axis=1)
        high = spec.astype(jnp.bfloat16)
        low = (spec - high.astype(jnp.float32)).astype(jnp.bfloat16)
        dot = functools.partial(jnp.dot, preferred_element_type=jnp.float32)
        block = dot(back_high[...], high) + dot(back_high[...], low) + dot(back_low[...], high)
        emit(i, block[:, :width])
        emit(i + 1, block[:, width:])


def columns_kernel(chips, direct, length, part, arrays, *refs):
    blocks, rest = refs[:-2], refs[-2:]
    position = lax.axis_index("ctx")

    def put(out, row, j, k):
        columns = pl.ds(pl.multiple_of((position ^ k) * part, part), part)
        out[row : row + length] = arrays[j, :, columns]

    for core in range(2):
        row = 0
        for i, chip in enumerate(chips):
            for j in range(3):
                if i < direct and j < 2:
                    put(blocks[2 * i + core], j * length, j, 2 * chip + core)
                else:
                    put(rest[core], row, j, 2 * chip + core)
                    row += length


def taps_kernel(rows, length, mine, sibling, *refs):
    tables, messages, held = refs[:3], refs[3:-3], refs[-3:]
    for table, place in zip(tables, held):
        place[...] = table[...]
    for row, message in zip(rows, messages):
        message[:length] = mine[row : row + length]
        message[length:] = sibling[row : row + length]


def first_kernel(order, length, places, *refs):
    size = len(order)
    both, back_high, back_low, blocks_out, skip_out, pair_spec, squares, spec, acc = refs[-9:]
    width = spec.shape[2] // 2
    position = lax.axis_index("ctx")

    skip = jnp.zeros((1, width), jnp.float32)
    for i, k in enumerate(order):
        ref, row = places[i]
        grad, other = refs[ref][row : row + length], refs[ref][row + length : row + 2 * length]
        skip += jnp.sum(grad.astype(jnp.float32) * other.astype(jnp.float32), axis=0, keepdims=True)
        lanes = jnp.concatenate([grad, other], axis=1)
        spec[position ^ k] = jnp.dot(
            both[...], jnp.concatenate([lanes, lanes], axis=0), preferred_element_type=jnp.float32
        )

    flip = jnp.where(lax.broadcasted_iota(jnp.int32, (8, width), 0) % 2 == 0, 1.0, -1.0)

    def rows(r, carry):
        real_rows = pl.ds(pl.multiple_of(r * 8, 8), 8)
        imag_rows = pl.ds(pl.multiple_of(length + r * 8, 8), 8)
        grad = [(spec[q, real_rows, :width], spec[q, imag_rows, :width]) for q in range(size)]
        pairs = []
        for q in range(size):
            if q + 1 < size:
                real = grad[q][0] + flip * grad[q + 1][1]
                imag = grad[q][1] - flip * grad[q + 1][0]
            else:
                real, imag = grad[q]
            pair_spec[q, real_rows, :] = real
            pair_spec[q, imag_rows, :] = imag
            pairs.append((real, imag))
        others = [(spec[q, real_rows, width:], spec[q, imag_rows, width:]) for q in range(size)]
        for p, (real, imag) in enumerate(correlate_rows(pairs, others, size)):
            acc[p, real_rows, :] = real
            acc[p, imag_rows, :] = imag
        return carry

    lax.fori_loop(0, length // 8, rows, 0)
    skip_out[...] = skip
    squares[...] = jnp.zeros_like(squares)

    def emit(i, block):
        squares[...] += jnp.sum((block * block).reshape(length // 8, 8, width), axis=0)
        blocks_out[i] = block

    send_results(position, order, acc, back_high, back_low, emit)


def second_kernel(order, length, places, *refs):
    size = len(order)
    both, back_high, back_low, pair_spec, blocks, skip = refs[-12:-6]
    filter_codes, filter_tails, input_codes, input_tails, spec, acc = refs[-6:]
    width = spec.shape[2]
    position = lax.axis_index("ctx")

    for i in range(0, size, 2):
        lanes = jnp.concatenate(
            [refs[ref][row : row + length] for ref, row in places[i : i + 2]], axis=1
        )
        both_specs = jnp.dot(
            both[...], jnp.concatenate([lanes, lanes], axis=0), preferred_element_type=jnp.float32
        )
        spec[position ^ order[i]] = both_specs[:, :width]
        spec[position ^ order[i + 1]] = both_specs[:, width:]

    def rows(r, carry):
        real_rows = pl.ds(pl.multiple_of(r * 8, 8), 8)
        imag_rows = pl.ds(pl.multiple_of(length + r * 8, 8), 8)
        pairs = [(pair_spec[q, real_rows, :], pair_spec[q, imag_rows, :]) for q in range(size)]
        others = [(spec[q, real_rows, :], spec[q, imag_rows, :]) for q in range(size)]
        for p, (real, imag) in enumerate(correlate_rows(pairs, others, size)):
            acc[p, real_rows, :] = real
            acc[p, imag_rows, :] = imag
        return carry

    lax.fori_loop(0, length // 8, rows, 0)

    skip_parts = three_parts(skip[...])
    for i in range(size):
        filter_codes[i], scale = encode(blocks[i])
        filter_tails[i] = tail_tile(0, (scale,) + skip_parts, width)

    def emit(i, block):
        input_codes[i], scale = encode(block)
        input_tails[i] = tail_tile(4, (scale,), width)

    send_results(position, order, acc, back_high, back_low, emit)


def message_kernel(size, length, sums, *refs):
    filter_codes, filter_tails, input_codes, input_tails = refs[:4]
    partial_squares, out = refs[4 : 4 + sums], refs[4 + sums :]
    squares = partial_squares[0][...]
    for other in partial_squares[1:]:
        squares += other[...]
    total = jnp.sum(jnp.sum(squares, axis=0, keepdims=True), axis=1, keepdims=True)
    total = jnp.minimum(total, 3.38e38)
    width = squares.shape[1]
    total_rows = tail_tile(5, three_parts(jnp.broadcast_to(total, (1, width))), width)
    for i in range(size):
        out[i][:length] = filter_codes[i]
        out[i][length : 2 * length] = input_codes[i]
        tail = filter_tails[i] + input_tails[i] + total_rows
        out[i][2 * length :] = tail.astype(jnp.bfloat16)


def early_kernel(order, length, part, *refs):
    messages, (grad, gain, input_blocks, filter_blocks) = refs[:-4], refs[-4:]
    position = lax.axis_index("ctx")
    for i, (k, message) in enumerate(zip(order, messages)):
        columns = pl.ds(pl.multiple_of((position ^ k) * part, part), part)
        tail = message[2 * length :].astype(jnp.float32)
        filter_blocks[i] = decode(message[:length], tail[0:1])
        input_blocks[i] = (
            decode(message[length : 2 * length], tail[4:5])
            + gain[:, columns] * grad[:, columns].astype(jnp.float32)
        )


def last_kernel(order, early, length, part, clip_limit, *refs):
    size = len(order)
    messages = refs[:size]
    input_blocks, filter_blocks, grad, gain, input_grad, filter_grad, skip_grad = refs[size:]
    position = lax.axis_index("ctx")
    total = jnp.zeros((1, part), jnp.float32)
    for message in messages:
        tail = message[2 * length :].astype(jnp.float32)
        total += tail[5:6] + tail[6:7] + tail[7:8]
    factor = jnp.minimum(1.0, clip_limit / jnp.sqrt(total + epsilon))
    for i, (k, message) in enumerate(zip(order, messages)):
        columns = pl.ds(pl.multiple_of((position ^ k) * part, part), part)
        tail = message[2 * length :].astype(jnp.float32)
        skip_grad[:, columns] = tail[1:2] + tail[2:3] + tail[3:4]
        if i < early:
            filter_grad[:, columns] = filter_blocks[i] * factor
            input_grad[:, columns] = input_blocks[i]
        else:
            filter_grad[:, columns] = decode(message[:length], tail[0:1]) * factor
            input_grad[:, columns] = (
                decode(message[length : 2 * length], tail[4:5])
                + gain[:, columns] * grad[:, columns].astype(jnp.float32)
            )


def run(kernel, name, vmem_bytes, out_shape, scratch=(), flops=10**9, **specs):
    return pl.pallas_call(
        kernel,
        out_shape=out_shape,
        scratch_shapes=scratch,
        name=name,
        **specs,
        cost_estimate=pl.CostEstimate(flops=flops, bytes_accessed=0, transcendentals=0),
        compiler_params=pltpu.CompilerParams(vmem_limit_bytes=vmem_bytes),
    )


def per_device(inputs, filter_taps, out_grad, skip_gain):
    length, chan_width = inputs.shape
    size = lax.axis_size("ctx")
    columns = lax.axis_size("chan")
    part = chan_width // size
    width = -(-part // 128) * 128
    position = lax.axis_index("ctx")
    both, back_high, back_low = tables(length)
    f32, bf16 = jnp.float32, jnp.bfloat16
    chips = sorted(range(size // 2), key=lambda chip: (-chip.bit_length(), -chip))
    order = [k for chip in chips for k in (2 * chip, 2 * chip + 1)]
    far = size // 4
    vmem_bytes = (8 + size) * 2**20

    def columns_for(array, k):
        block = lax.dynamic_slice_in_dim(array, (position ^ k) * part, part, 1)
        return jnp.pad(block, ((0, 0), (0, width - part)))

    def send(block, k):
        return lax.ppermute(block, "ctx", [(i, i ^ k) for i in range(size)])

    three = (out_grad, inputs, filter_taps)
    direct = size // 8
    rest_rows = (3 * len(chips) - 2 * direct) * length
    if width == part:
        *blocks, mine, others = run(
            functools.partial(columns_kernel, chips, direct, length, part),
            "columns", vmem_bytes,
            [jax.ShapeDtypeStruct((2 * length, width), bf16)] * (2 * direct)
            + [jax.ShapeDtypeStruct((rest_rows, width), bf16)] * 2,
        )(jnp.stack(three))
    else:
        blocks = [jnp.concatenate([columns_for(a, k) for a in three[:2]]) for k in order[: 2 * direct]]
        mine, others = (
            jnp.concatenate(
                [
                    columns_for(a, 2 * chip + core)
                    for i, chip in enumerate(chips)
                    for a in (three[2:] if i < direct else three)
                ]
            )
            for core in range(2)
        )

    sibling = send(others, 1)
    arrived = [send(block, k) for k, block in zip(order, blocks)]
    first_places = [(i, 0) for i in range(2 * direct)]
    taps_rows = [i * length for i in range(direct)]
    row = direct * length
    near_places = []
    for i, chip in enumerate(chips[direct:-1]):
        here = len(arrived)
        rows = (2 if i < far - direct else 3) * length
        pair = jnp.concatenate([held[row : row + rows] for held in (mine, sibling)])
        first_places += [(here, 0), (here, rows)]
        arrived.append(send(pair, 2 * chip))
        if i < far - direct:
            taps_rows.append(row + 2 * length)
        else:
            near_places += [(here, 2 * length), (here, 5 * length)]
        row += 3 * length
    first_places += [(len(arrived), row), (len(arrived) + 1, row)]
    first_arrived = [*arrived, mine, sibling]
    later = lax.optimization_barrier((mine, sibling, *arrived[: 2 * direct]))[:2]
    *tap_messages, both, back_high, back_low = run(
        functools.partial(taps_kernel, taps_rows, length),
        "taps", vmem_bytes,
        [jax.ShapeDtypeStruct((2 * length, width), bf16)] * len(taps_rows)
        + [jax.ShapeDtypeStruct(t.shape, t.dtype) for t in (both, back_high, back_low)],
    )(*later, both, back_high, back_low)
    arrived_taps = [send(block, 2 * chip) for chip, block in zip(chips, tap_messages)]
    second_places = [(i, half) for i in range(far) for half in (0, length)]
    second_places += [(ref - 2 * direct - (far - direct) + far, at) for ref, at in near_places]
    second_arrived = [*arrived_taps, *arrived[direct + far :], mine, sibling]
    second_places += [(len(second_arrived) - 2 + i, row + 2 * length) for i in range(2)]

    filter_blocks, skip, pair_spec, squares = run(
        functools.partial(first_kernel, order, length, first_places),
        "filter_gradient", vmem_bytes,
        [
            jax.ShapeDtypeStruct((size, length, width), f32),
            jax.ShapeDtypeStruct((1, width), f32),
            jax.ShapeDtypeStruct((size, 2 * length, width), f32),
            jax.ShapeDtypeStruct((8, width), f32),
        ],
        [
            pltpu.VMEM((size, 2 * length, 2 * width), f32),
            pltpu.VMEM((size, 2 * length, width), f32),
        ],
        flops=first_flops,
    )(*first_arrived, both, back_high, back_low)
    all_squares = [
        squares if k == 0 else lax.ppermute(squares, "chan", [(i, i ^ k) for i in range(columns)])
        for k in range(columns)
    ]
    codes_and_tails = run(
        functools.partial(second_kernel, order, length, second_places),
        "input_gradient", vmem_bytes,
        [
            jax.ShapeDtypeStruct((size, length, width), bf16),
            jax.ShapeDtypeStruct((size, tail_rows, width), f32),
        ]
        * 2,
        [
            pltpu.VMEM((size, 2 * length, width), f32),
            pltpu.VMEM((size, 2 * length, width), f32),
        ],
        flops=second_flops,
    )(*second_arrived, both, back_high, back_low, pair_spec, filter_blocks, skip)
    messages = run(
        functools.partial(message_kernel, size, length, columns),
        "messages", vmem_bytes,
        [jax.ShapeDtypeStruct((2 * length + tail_rows, width), bf16)] * size,
    )(*codes_and_tails, *all_squares)
    messages = {k: send(message, k) if k else message for k, message in zip(order, messages)}
    nearer = sorted(chips[:far])
    turns = nearer[: far // 2] + chips[far:-1] + nearer[far // 2 :] + [0]
    turns = [k for chip in turns for k in (2 * chip, 2 * chip + 1)]

    clip_limit = 0.25 * math.sqrt(length * size * chan_width * columns)
    whole = size * width
    grad_rows, gain = out_grad, skip_gain[None, :]
    if width != part:
        spread = lambda a: jnp.pad(
            a.reshape(a.shape[0], size, part), ((0, 0), (0, 0), (0, width - part))
        ).reshape(a.shape[0], whole)
        grad_rows, gain = spread(grad_rows), spread(gain)
    turns = turns[: size // 2] + [0] + [k for k in turns[size // 2 :] if k]
    early = size // 2 + 1
    decoded = run(
        functools.partial(early_kernel, turns[:early], length, width),
        "early", vmem_bytes,
        [jax.ShapeDtypeStruct((early, length, width), f32)] * 2,
        flops=first_flops,
    )(*[messages[k] for k in turns[:early]], grad_rows, gain)
    input_grad, filter_grad, skip_grad = run(
        functools.partial(last_kernel, turns, early, length, width, clip_limit),
        "outputs", vmem_bytes,
        [
            jax.ShapeDtypeStruct((length, whole), f32),
            jax.ShapeDtypeStruct((length, whole), f32),
            jax.ShapeDtypeStruct((1, whole), f32),
        ],
    )(*[messages[k] for k in turns], *decoded, grad_rows, gain)
    if width != part:
        gather = lambda a: a.reshape(a.shape[0], size, width)[:, :, :part].reshape(
            a.shape[0], chan_width
        )
        input_grad, filter_grad, skip_grad = gather(input_grad), gather(filter_grad), gather(skip_grad)
    return (input_grad, filter_grad, skip_grad[0])


def solution(mesh):
    return jax.shard_map(
        per_device,
        mesh=mesh,
        in_specs=(P("ctx", "chan"), P("ctx", "chan"), P("ctx", "chan"), P("chan")),
        out_specs=(P("ctx", "chan"), P("ctx", "chan"), P("chan")),
        check_vma=False,
    )
```

```python
import functools
import math

import jax
import jax.numpy as jnp
import numpy as np
from jax import lax
from jax.experimental import pallas as pl
from jax.experimental.pallas import tpu as pltpu
from jax.sharding import PartitionSpec as P

epsilon = 1e-06
octaves = 246
low_power = 120
top_code = 128 * octaves - 1
tail_rows = 16
first_flops = 4 * 10**9
second_flops = 2 * 10**10


def tables(length):
    odd = 2 * np.arange(length) + 1
    phase = odd[:, None] * np.arange(length)[None, :] % (4 * length)
    angles = np.pi * phase / (2 * length)
    forward = np.concatenate([np.cos(angles), -np.sin(angles)], axis=0)
    high = forward.astype(np.float32).astype(jnp.bfloat16)
    low = (forward - high.astype(np.float64)).astype(np.float32).astype(jnp.bfloat16)
    both = np.concatenate([high, low], axis=1)
    scale = np.float32(1.0 / length)
    back_high = (high.astype(np.float32).T * scale).astype(jnp.bfloat16)
    back_low = (low.astype(np.float32).T * scale).astype(jnp.bfloat16)
    return jnp.asarray(both), jnp.asarray(back_high), jnp.asarray(back_low)


def three_parts(value):
    high = value.astype(jnp.bfloat16).astype(jnp.float32)
    rest = value - high
    middle = rest.astype(jnp.bfloat16).astype(jnp.float32)
    return high, middle, rest - middle


def encode(values):
    peak = jnp.max(jnp.abs(values), axis=0, keepdims=True) * (1.0 + 2.0**-7)
    scale = jnp.maximum(peak.astype(jnp.bfloat16).astype(jnp.float32), 2.0**-116)
    size = jnp.abs(values) * (top_code / 128.0 / scale)
    octave = jnp.floor(size)
    carrier = (size - octave + 1.0) * jnp.exp2(octave - float(low_power))
    return jnp.where(values < 0, -carrier, carrier).astype(jnp.bfloat16), scale


def decode(codes, scale):
    carrier = codes.astype(jnp.float32)
    size = jnp.abs(carrier)
    power = jnp.floor(jnp.log2(size) + 0.001)
    octaves_up = size * jnp.exp2(-power) + (power + float(low_power - 1))
    scale *= 128.0 / top_code
    return octaves_up * jnp.where(carrier < 0, -scale, scale)


def tail_tile(first_row, rows, width):
    row_ids = lax.broadcasted_iota(jnp.int32, (tail_rows, width), 0)
    tile = jnp.zeros((tail_rows, width), jnp.float32)
    for i, row in enumerate(rows):
        tile = jnp.where(
            row_ids == first_row + i, jnp.broadcast_to(row, (tail_rows, width)), tile
        )
    return tile


def correlate_rows(pairs, others, size):
    sums = [real + imag for real, imag in pairs]
    turned = [(real, real - imag, real + imag) for real, imag in others]
    results = []
    for p in range(size):
        shared = first = second = None
        for q in range(p, size):
            real, less, more = turned[q - p]
            terms = sums[q] * real, pairs[q][1] * less, pairs[q][0] * more
            if q > p:
                terms = shared + terms[0], first + terms[1], second + terms[2]
            shared, first, second = terms
        results.append((shared - first, shared - second))
    return results


def send_results(position, order, acc, back_high, back_low, emit):
    width = acc.shape[2]
    for i in range(0, len(order), 2):
        spec = jnp.concatenate([acc[position ^ order[i]], acc[position ^ order[i + 1]]], axis=1)
        high = spec.astype(jnp.bfloat16)
        low = (spec - high.astype(jnp.float32)).astype(jnp.bfloat16)
        dot = functools.partial(jnp.dot, preferred_element_type=jnp.float32)
        block = dot(back_high[...], high) + dot(back_high[...], low) + dot(back_low[...], high)
        emit(i, block[:, :width])
        emit(i + 1, block[:, width:])


def columns_kernel(chips, direct, length, part, *refs):
    halves, blocks, rest = refs[:6], refs[6:-2], refs[-2:]
    position = lax.axis_index("ctx")
    half = len(chips)

    def put(out, row, j, k):
        columns = pl.ds(pl.multiple_of((position ^ k) % half * part, part), part)
        out[row : row + length] = halves[2 * j + k // half][:, columns]

    for core in range(2):
        row = 0
        for i, chip in enumerate(chips):
            for j in range(3):
                if i < direct and j < 2:
                    put(blocks[2 * i + core], j * length, j, 2 * chip + core)
                else:
                    put(rest[core], row, j, 2 * chip + core)
                    row += length


def taps_kernel(rows, length, mine, sibling, *refs):
    tables, messages, held = refs[:3], refs[3:-3], refs[-3:]
    for table, place in zip(tables, held):
        place[...] = table[...]
    for row, message in zip(rows, messages):
        message[:length] = mine[row : row + length]
        message[length:] = sibling[row : row + length]


def first_kernel(order, length, places, *refs):
    size = len(order)
    both, back_high, back_low, blocks_out, skip_out, pair_spec, squares, spec, acc = refs[-9:]
    width = spec.shape[2] // 2
    position = lax.axis_index("ctx")

    skip = jnp.zeros((1, width), jnp.float32)
    for i, k in enumerate(order):
        ref, row = places[i]
        grad, other = refs[ref][row : row + length], refs[ref][row + length : row + 2 * length]
        skip += jnp.sum(grad.astype(jnp.float32) * other.astype(jnp.float32), axis=0, keepdims=True)
        lanes = jnp.concatenate([grad, other], axis=1)
        spec[position ^ k] = jnp.dot(
            both[...], jnp.concatenate([lanes, lanes], axis=0), preferred_element_type=jnp.float32
        )

    flip = jnp.where(lax.broadcasted_iota(jnp.int32, (8, width), 0) % 2 == 0, 1.0, -1.0)

    def rows(r, carry):
        real_rows = pl.ds(pl.multiple_of(r * 8, 8), 8)
        imag_rows = pl.ds(pl.multiple_of(length + r * 8, 8), 8)
        grad = [(spec[q, real_rows, :width], spec[q, imag_rows, :width]) for q in range(size)]
        pairs = []
        for q in range(size):
            if q + 1 < size:
                real = grad[q][0] + flip * grad[q + 1][1]
                imag = grad[q][1] - flip * grad[q + 1][0]
            else:
                real, imag = grad[q]
            pair_spec[q, real_rows, :] = real
            pair_spec[q, imag_rows, :] = imag
            pairs.append((real, imag))
        others = [(spec[q, real_rows, width:], spec[q, imag_rows, width:]) for q in range(size)]
        for p, (real, imag) in enumerate(correlate_rows(pairs, others, size)):
            acc[p, real_rows, :] = real
            acc[p, imag_rows, :] = imag
        return carry

    lax.fori_loop(0, length // 8, rows, 0, unroll=2)
    skip_out[...] = skip
    squares[...] = jnp.zeros_like(squares)

    def emit(i, block):
        squares[...] += jnp.sum((block * block).reshape(length // 8, 8, width), axis=0)
        blocks_out[i] = block

    send_results(position, order, acc, back_high, back_low, emit)


def second_kernel(order, length, places, *refs):
    size = len(order)
    both, back_high, back_low, pair_spec, blocks, skip = refs[-12:-6]
    filter_codes, filter_tails, input_codes, input_tails, spec, acc = refs[-6:]
    width = spec.shape[2]
    position = lax.axis_index("ctx")

    for i in range(0, size, 2):
        lanes = jnp.concatenate(
            [refs[ref][row : row + length] for ref, row in places[i : i + 2]], axis=1
        )
        both_specs = jnp.dot(
            both[...], jnp.concatenate([lanes, lanes], axis=0), preferred_element_type=jnp.float32
        )
        spec[position ^ order[i]] = both_specs[:, :width]
        spec[position ^ order[i + 1]] = both_specs[:, width:]

    def rows(r, carry):
        real_rows = pl.ds(pl.multiple_of(r * 8, 8), 8)
        imag_rows = pl.ds(pl.multiple_of(length + r * 8, 8), 8)
        pairs = [(pair_spec[q, real_rows, :], pair_spec[q, imag_rows, :]) for q in range(size)]
        others = [(spec[q, real_rows, :], spec[q, imag_rows, :]) for q in range(size)]
        for p, (real, imag) in enumerate(correlate_rows(pairs, others, size)):
            acc[p, real_rows, :] = real
            acc[p, imag_rows, :] = imag
        return carry

    lax.fori_loop(0, length // 8, rows, 0, unroll=2)

    skip_parts = three_parts(skip[...])
    for i in range(size):
        filter_codes[i], scale = encode(blocks[i])
        filter_tails[i] = tail_tile(0, (scale,) + skip_parts, width)

    def emit(i, block):
        input_codes[i], scale = encode(block)
        input_tails[i] = tail_tile(4, (scale,), width)

    send_results(position, order, acc, back_high, back_low, emit)


def message_kernel(size, length, sums, *refs):
    filter_codes, filter_tails, input_codes, input_tails = refs[:4]
    partial_squares, out = refs[4 : 4 + sums], refs[4 + sums :]
    squares = partial_squares[0][...]
    for other in partial_squares[1:]:
        squares += other[...]
    total = jnp.sum(jnp.sum(squares, axis=0, keepdims=True), axis=1, keepdims=True)
    total = jnp.minimum(total, 3.38e38)
    width = squares.shape[1]
    total_rows = tail_tile(5, three_parts(jnp.broadcast_to(total, (1, width))), width)
    for i in range(size):
        out[i][:length] = filter_codes[i]
        out[i][length : 2 * length] = input_codes[i]
        tail = filter_tails[i] + input_tails[i] + total_rows
        out[i][2 * length :] = tail.astype(jnp.bfloat16)


def early_kernel(order, length, part, *refs):
    messages, (grad, gain, input_blocks, filter_blocks) = refs[:-4], refs[-4:]
    position = lax.axis_index("ctx")
    for i, (k, message) in enumerate(zip(order, messages)):
        columns = pl.ds(pl.multiple_of((position ^ k) * part, part), part)
        tail = message[2 * length :].astype(jnp.float32)
        filter_blocks[i] = decode(message[:length], tail[0:1])
        input_blocks[i] = (
            decode(message[length : 2 * length], tail[4:5])
            + gain[:, columns] * grad[:, columns].astype(jnp.float32)
        )


def last_kernel(order, early, length, part, clip_limit, *refs):
    size = len(order)
    messages = refs[:size]
    input_blocks, filter_blocks, grad, gain, input_grad, filter_grad, skip_grad = refs[size:]
    position = lax.axis_index("ctx")
    total = jnp.zeros((1, part), jnp.float32)
    for message in messages:
        tail = message[2 * length :].astype(jnp.float32)
        total += tail[5:6] + tail[6:7] + tail[7:8]
    factor = jnp.minimum(1.0, clip_limit / jnp.sqrt(total + epsilon))
    for i, (k, message) in enumerate(zip(order, messages)):
        columns = pl.ds(pl.multiple_of((position ^ k) * part, part), part)
        tail = message[2 * length :].astype(jnp.float32)
        skip_grad[:, columns] = tail[1:2] + tail[2:3] + tail[3:4]
        if i < early:
            filter_grad[:, columns] = filter_blocks[i] * factor
            input_grad[:, columns] = input_blocks[i]
        else:
            filter_grad[:, columns] = decode(message[:length], tail[0:1]) * factor
            input_grad[:, columns] = (
                decode(message[length : 2 * length], tail[4:5])
                + gain[:, columns] * grad[:, columns].astype(jnp.float32)
            )


def run(kernel, name, vmem_bytes, out_shape, scratch=(), flops=10**9, **specs):
    return pl.pallas_call(
        kernel,
        out_shape=out_shape,
        scratch_shapes=scratch,
        name=name,
        **specs,
        cost_estimate=pl.CostEstimate(flops=flops, bytes_accessed=0, transcendentals=0),
        compiler_params=pltpu.CompilerParams(vmem_limit_bytes=vmem_bytes),
    )


def per_device(inputs, filter_taps, out_grad, skip_gain):
    length, chan_width = inputs.shape
    size = lax.axis_size("ctx")
    columns = lax.axis_size("chan")
    part = chan_width // size
    width = -(-part // 128) * 128
    position = lax.axis_index("ctx")
    both, back_high, back_low = tables(length)
    f32, bf16 = jnp.float32, jnp.bfloat16
    chips = sorted(range(size // 2), key=lambda chip: (-chip.bit_length(), -chip))
    order = [k for chip in chips for k in (2 * chip, 2 * chip + 1)]
    far = size // 4
    vmem_bytes = (8 + size) * 2**20

    def columns_for(array, k):
        block = lax.dynamic_slice_in_dim(array, (position ^ k) * part, part, 1)
        return jnp.pad(block, ((0, 0), (0, width - part)))

    def send(block, k):
        return lax.ppermute(block, "ctx", [(i, i ^ k) for i in range(size)])

    three = (out_grad, inputs, filter_taps)
    direct = size // 8
    rest_rows = (3 * len(chips) - 2 * direct) * length
    half = size // 2
    if width == part:
        *blocks, mine, others = run(
            functools.partial(columns_kernel, chips, direct, length, part),
            "columns", vmem_bytes,
            [jax.ShapeDtypeStruct((2 * length, width), bf16)] * (2 * direct)
            + [jax.ShapeDtypeStruct((rest_rows, width), bf16)] * 2,
        )(*[
            lax.dynamic_slice_in_dim(array, (position // half * half ^ other) * part, half * part, 1)
            for array in three
            for other in (0, half)
        ])
    else:
        blocks = [jnp.concatenate([columns_for(a, k) for a in three[:2]]) for k in order[: 2 * direct]]
        mine, others = (
            jnp.concatenate(
                [
                    columns_for(a, 2 * chip + core)
                    for i, chip in enumerate(chips)
                    for a in (three[2:] if i < direct else three)
                ]
            )
            for core in range(2)
        )

    sibling = send(others, 1)
    arrived = [send(block, k) for k, block in zip(order, blocks)]
    first_places = [(i, 0) for i in range(2 * direct)]
    taps_rows = [i * length for i in range(direct)]
    row = direct * length
    near_places = []
    for i, chip in enumerate(chips[direct:-1]):
        here = len(arrived)
        rows = (2 if i < far - direct else 3) * length
        pair = jnp.concatenate([held[row : row + rows] for held in (mine, sibling)])
        first_places += [(here, 0), (here, rows)]
        arrived.append(send(pair, 2 * chip))
        if i < far - direct:
            taps_rows.append(row + 2 * length)
        else:
            near_places += [(here, 2 * length), (here, 5 * length)]
        row += 3 * length
    first_places += [(len(arrived), row), (len(arrived) + 1, row)]
    first_arrived = [*arrived, mine, sibling]
    later = lax.optimization_barrier((mine, sibling, *arrived[: 2 * direct]))[:2]
    *tap_messages, both, back_high, back_low = run(
        functools.partial(taps_kernel, taps_rows, length),
        "taps", vmem_bytes,
        [jax.ShapeDtypeStruct((2 * length, width), bf16)] * len(taps_rows)
        + [jax.ShapeDtypeStruct(t.shape, t.dtype) for t in (both, back_high, back_low)],
    )(*later, both, back_high, back_low)
    arrived_taps = [send(block, 2 * chip) for chip, block in zip(chips, tap_messages)]
    second_places = [(i, half) for i in range(far) for half in (0, length)]
    second_places += [(ref - 2 * direct - (far - direct) + far, at) for ref, at in near_places]
    second_arrived = [*arrived_taps, *arrived[direct + far :], mine, sibling]
    second_places += [(len(second_arrived) - 2 + i, row + 2 * length) for i in range(2)]

    filter_blocks, skip, pair_spec, squares = run(
        functools.partial(first_kernel, order, length, first_places),
        "filter_gradient", vmem_bytes,
        [
            jax.ShapeDtypeStruct((size, length, width), f32),
            jax.ShapeDtypeStruct((1, width), f32),
            jax.ShapeDtypeStruct((size, 2 * length, width), f32),
            jax.ShapeDtypeStruct((8, width), f32),
        ],
        [
            pltpu.VMEM((size, 2 * length, 2 * width), f32),
            pltpu.VMEM((size, 2 * length, width), f32),
        ],
        flops=first_flops,
    )(*first_arrived, both, back_high, back_low)
    all_squares = [
        squares if k == 0 else lax.ppermute(squares, "chan", [(i, i ^ k) for i in range(columns)])
        for k in range(columns)
    ]
    codes_and_tails = run(
        functools.partial(second_kernel, order, length, second_places),
        "input_gradient", vmem_bytes,
        [
            jax.ShapeDtypeStruct((size, length, width), bf16),
            jax.ShapeDtypeStruct((size, tail_rows, width), f32),
        ]
        * 2,
        [
            pltpu.VMEM((size, 2 * length, width), f32),
            pltpu.VMEM((size, 2 * length, width), f32),
        ],
        flops=second_flops,
    )(*second_arrived, both, back_high, back_low, pair_spec, filter_blocks, skip)
    messages = run(
        functools.partial(message_kernel, size, length, columns),
        "messages", vmem_bytes,
        [jax.ShapeDtypeStruct((2 * length + tail_rows, width), bf16)] * size,
    )(*codes_and_tails, *all_squares)
    messages = {k: send(message, k) if k else message for k, message in zip(order, messages)}
    nearer = sorted(chips[:far])
    turns = nearer[: far // 2] + chips[far:-1] + nearer[far // 2 :] + [0]
    turns = [k for chip in turns for k in (2 * chip, 2 * chip + 1)]

    clip_limit = 0.25 * math.sqrt(length * size * chan_width * columns)
    whole = size * width
    grad_rows, gain = out_grad, skip_gain[None, :]
    if width != part:
        spread = lambda a: jnp.pad(
            a.reshape(a.shape[0], size, part), ((0, 0), (0, 0), (0, width - part))
        ).reshape(a.shape[0], whole)
        grad_rows, gain = spread(grad_rows), spread(gain)
    turns = turns[: size // 2] + [0] + [k for k in turns[size // 2 :] if k]
    early = size // 2 + 1
    decoded = run(
        functools.partial(early_kernel, turns[:early], length, width),
        "early", vmem_bytes,
        [jax.ShapeDtypeStruct((early, length, width), f32)] * 2,
        flops=first_flops,
    )(*[messages[k] for k in turns[:early]], grad_rows, gain)
    input_grad, filter_grad, skip_grad = run(
        functools.partial(last_kernel, turns, early, length, width, clip_limit),
        "outputs", vmem_bytes,
        [
            jax.ShapeDtypeStruct((length, whole), f32),
            jax.ShapeDtypeStruct((length, whole), f32),
            jax.ShapeDtypeStruct((1, whole), f32),
        ],
    )(*[messages[k] for k in turns], *decoded, grad_rows, gain)
    if width != part:
        gather = lambda a: a.reshape(a.shape[0], size, width)[:, :, :part].reshape(
            a.shape[0], chan_width
        )
        input_grad, filter_grad, skip_grad = gather(input_grad), gather(filter_grad), gather(skip_grad)
    return (input_grad, filter_grad, skip_grad[0])


def solution(mesh):
    return jax.shard_map(
        per_device,
        mesh=mesh,
        in_specs=(P("ctx", "chan"), P("ctx", "chan"), P("ctx", "chan"), P("chan")),
        out_specs=(P("ctx", "chan"), P("ctx", "chan"), P("chan")),
        check_vma=False,
    )
```

```python
import functools
import math

import jax
import jax.numpy as jnp
import numpy as np
from jax import lax
from jax.experimental import pallas as pl
from jax.experimental.pallas import tpu as pltpu
from jax.sharding import PartitionSpec as P

epsilon = 1e-06
octaves = 246
low_power = 120
top_code = 128 * octaves - 1
tail_rows = 16
first_flops = 4 * 10**9
second_flops = 2 * 10**10


def tables(length):
    odd = 2 * np.arange(length) + 1
    phase = odd[:, None] * np.arange(length)[None, :] % (4 * length)
    angles = np.pi * phase / (2 * length)
    forward = np.concatenate([np.cos(angles), -np.sin(angles)], axis=0)
    high = forward.astype(np.float32).astype(jnp.bfloat16)
    low = (forward - high.astype(np.float64)).astype(np.float32).astype(jnp.bfloat16)
    both = np.concatenate([high, low], axis=1)
    scale = np.float32(1.0 / length)
    back_high = (high.astype(np.float32).T * scale).astype(jnp.bfloat16)
    back_low = (low.astype(np.float32).T * scale).astype(jnp.bfloat16)
    return jnp.asarray(both), jnp.asarray(back_high), jnp.asarray(back_low)


def three_parts(value):
    high = value.astype(jnp.bfloat16).astype(jnp.float32)
    rest = value - high
    middle = rest.astype(jnp.bfloat16).astype(jnp.float32)
    return high, middle, rest - middle


def encode(values):
    peak = jnp.max(jnp.abs(values), axis=0, keepdims=True) * (1.0 + 2.0**-7)
    scale = jnp.maximum(peak.astype(jnp.bfloat16).astype(jnp.float32), 2.0**-116)
    size = jnp.abs(values) * (top_code / 128.0 / scale)
    octave = jnp.floor(size)
    carrier = (size - octave + 1.0) * jnp.exp2(octave - float(low_power))
    return jnp.where(values < 0, -carrier, carrier).astype(jnp.bfloat16), scale


def decode(codes, scale):
    carrier = codes.astype(jnp.float32)
    size = jnp.abs(carrier)
    power = jnp.floor(jnp.log2(size) + 0.001)
    octaves_up = size * jnp.exp2(-power) + (power + float(low_power - 1))
    scale *= 128.0 / top_code
    return octaves_up * jnp.where(carrier < 0, -scale, scale)


def tail_tile(first_row, rows, width):
    row_ids = lax.broadcasted_iota(jnp.int32, (tail_rows, width), 0)
    tile = jnp.zeros((tail_rows, width), jnp.float32)
    for i, row in enumerate(rows):
        tile = jnp.where(
            row_ids == first_row + i, jnp.broadcast_to(row, (tail_rows, width)), tile
        )
    return tile


def correlate_rows(pairs, others, size):
    sums = [real + imag for real, imag in pairs]
    turned = [(real, real - imag, real + imag) for real, imag in others]
    results = []
    for p in range(size):
        shared = first = second = None
        for q in range(p, size):
            real, less, more = turned[q - p]
            terms = sums[q] * real, pairs[q][1] * less, pairs[q][0] * more
            if q > p:
                terms = shared + terms[0], first + terms[1], second + terms[2]
            shared, first, second = terms
        results.append((shared - first, shared - second))
    return results


def send_results(position, order, acc, back_high, back_low, emit):
    width = acc.shape[2]
    for i in range(0, len(order), 2):
        spec = jnp.concatenate([acc[position ^ order[i]], acc[position ^ order[i + 1]]], axis=1)
        high = spec.astype(jnp.bfloat16)
        low = (spec - high.astype(jnp.float32)).astype(jnp.bfloat16)
        dot = functools.partial(jnp.dot, preferred_element_type=jnp.float32)
        block = dot(back_high[...], high) + dot(back_high[...], low) + dot(back_low[...], high)
        emit(i, block[:, :width])
        emit(i + 1, block[:, width:])


def columns_kernel(chips, direct, length, part, *refs):
    halves, blocks, rest = refs[:6], refs[6:-2], refs[-2:]
    position = lax.axis_index("ctx")
    half = len(chips)

    def put(out, row, j, k):
        columns = pl.ds(pl.multiple_of((position ^ k) % half * part, part), part)
        out[row : row + length] = halves[2 * j + k // half][:, columns]

    for core in range(2):
        row = 0
        for i, chip in enumerate(chips):
            for j in range(3):
                if i < direct and j < 2:
                    put(blocks[2 * i + core], j * length, j, 2 * chip + core)
                else:
                    put(rest[core], row, j, 2 * chip + core)
                    row += length


def taps_kernel(rows, length, mine, sibling, *refs):
    tables, messages, held = refs[:3], refs[3:-3], refs[-3:]
    for table, place in zip(tables, held):
        place[...] = table[...]
    for row, message in zip(rows, messages):
        message[:length] = mine[row : row + length]
        message[length:] = sibling[row : row + length]


def first_kernel(order, length, places, *refs):
    size = len(order)
    both, back_high, back_low, blocks_out, skip_out, pair_spec, squares, spec, acc = refs[-9:]
    width = spec.shape[2] // 2
    position = lax.axis_index("ctx")

    skip = jnp.zeros((1, width), jnp.float32)
    for i, k in enumerate(order):
        ref, row = places[i]
        grad, other = refs[ref][row : row + length], refs[ref][row + length : row + 2 * length]
        skip += jnp.sum(grad.astype(jnp.float32) * other.astype(jnp.float32), axis=0, keepdims=True)
        lanes = jnp.concatenate([grad, other], axis=1)
        spec[position ^ k] = jnp.dot(
            both[...], jnp.concatenate([lanes, lanes], axis=0), preferred_element_type=jnp.float32
        )

    flip = jnp.where(lax.broadcasted_iota(jnp.int32, (8, width), 0) % 2 == 0, 1.0, -1.0)

    def rows(r, carry):
        real_rows = pl.ds(pl.multiple_of(r * 8, 8), 8)
        imag_rows = pl.ds(pl.multiple_of(length + r * 8, 8), 8)
        grad = [(spec[q, real_rows, :width], spec[q, imag_rows, :width]) for q in range(size)]
        pairs = []
        for q in range(size):
            if q + 1 < size:
                real = grad[q][0] + flip * grad[q + 1][1]
                imag = grad[q][1] - flip * grad[q + 1][0]
            else:
                real, imag = grad[q]
            pair_spec[q, real_rows, :] = real
            pair_spec[q, imag_rows, :] = imag
            pairs.append((real, imag))
        others = [(spec[q, real_rows, width:], spec[q, imag_rows, width:]) for q in range(size)]
        for p, (real, imag) in enumerate(correlate_rows(pairs, others, size)):
            acc[p, real_rows, :] = real
            acc[p, imag_rows, :] = imag
        return carry

    lax.fori_loop(0, length // 8, rows, 0, unroll=2)
    skip_out[...] = skip
    squares[...] = jnp.zeros_like(squares)

    def emit(i, block):
        squares[...] += jnp.sum((block * block).reshape(length // 8, 8, width), axis=0)
        blocks_out[i] = block

    send_results(position, order, acc, back_high, back_low, emit)


def code_kernel(size, width, blocks, skip, filter_codes, filter_tails):
    skip_parts = three_parts(skip[...])
    for i in range(size):
        filter_codes[i], scale = encode(blocks[i])
        filter_tails[i] = tail_tile(0, (scale,) + skip_parts, width)


def second_kernel(order, length, places, *refs):
    size = len(order)
    both, back_high, back_low, pair_spec, input_codes, input_tails, spec, acc = refs[-8:]
    width = spec.shape[2]
    position = lax.axis_index("ctx")

    for i in range(0, size, 2):
        lanes = jnp.concatenate(
            [refs[ref][row : row + length] for ref, row in places[i : i + 2]], axis=1
        )
        both_specs = jnp.dot(
            both[...], jnp.concatenate([lanes, lanes], axis=0), preferred_element_type=jnp.float32
        )
        spec[position ^ order[i]] = both_specs[:, :width]
        spec[position ^ order[i + 1]] = both_specs[:, width:]

    def rows(r, carry):
        real_rows = pl.ds(pl.multiple_of(r * 8, 8), 8)
        imag_rows = pl.ds(pl.multiple_of(length + r * 8, 8), 8)
        pairs = [(pair_spec[q, real_rows, :], pair_spec[q, imag_rows, :]) for q in range(size)]
        others = [(spec[q, real_rows, :], spec[q, imag_rows, :]) for q in range(size)]
        for p, (real, imag) in enumerate(correlate_rows(pairs, others, size)):
            acc[p, real_rows, :] = real
            acc[p, imag_rows, :] = imag
        return carry

    lax.fori_loop(0, length // 8, rows, 0, unroll=2)

    def emit(i, block):
        input_codes[i], scale = encode(block)
        input_tails[i] = tail_tile(4, (scale,), width)

    send_results(position, order, acc, back_high, back_low, emit)


def message_kernel(size, length, sums, *refs):
    filter_codes, filter_tails, input_codes, input_tails = refs[:4]
    partial_squares, out = refs[4 : 4 + sums], refs[4 + sums :]
    squares = partial_squares[0][...]
    for other in partial_squares[1:]:
        squares += other[...]
    total = jnp.sum(jnp.sum(squares, axis=0, keepdims=True), axis=1, keepdims=True)
    total = jnp.minimum(total, 3.38e38)
    width = squares.shape[1]
    total_rows = tail_tile(5, three_parts(jnp.broadcast_to(total, (1, width))), width)
    for i in range(size):
        out[i][:length] = filter_codes[i]
        out[i][length : 2 * length] = input_codes[i]
        tail = filter_tails[i] + input_tails[i] + total_rows
        out[i][2 * length :] = tail.astype(jnp.bfloat16)


def early_kernel(order, length, part, *refs):
    messages, (grad, gain, input_blocks, filter_blocks) = refs[:-4], refs[-4:]
    position = lax.axis_index("ctx")
    for i, (k, message) in enumerate(zip(order, messages)):
        columns = pl.ds(pl.multiple_of((position ^ k) * part, part), part)
        tail = message[2 * length :].astype(jnp.float32)
        filter_blocks[i] = decode(message[:length], tail[0:1])
        input_blocks[i] = (
            decode(message[length : 2 * length], tail[4:5])
            + gain[:, columns] * grad[:, columns].astype(jnp.float32)
        )


def last_kernel(order, early, length, part, clip_limit, *refs):
    size = len(order)
    messages = refs[:size]
    input_blocks, filter_blocks, grad, gain, input_grad, filter_grad, skip_grad = refs[size:]
    position = lax.axis_index("ctx")
    total = jnp.zeros((1, part), jnp.float32)
    for message in messages:
        tail = message[2 * length :].astype(jnp.float32)
        total += tail[5:6] + tail[6:7] + tail[7:8]
    factor = jnp.minimum(1.0, clip_limit / jnp.sqrt(total + epsilon))
    for i, (k, message) in enumerate(zip(order, messages)):
        columns = pl.ds(pl.multiple_of((position ^ k) * part, part), part)
        tail = message[2 * length :].astype(jnp.float32)
        skip_grad[:, columns] = tail[1:2] + tail[2:3] + tail[3:4]
        if i < early:
            filter_grad[:, columns] = filter_blocks[i] * factor
            input_grad[:, columns] = input_blocks[i]
        else:
            filter_grad[:, columns] = decode(message[:length], tail[0:1]) * factor
            input_grad[:, columns] = (
                decode(message[length : 2 * length], tail[4:5])
                + gain[:, columns] * grad[:, columns].astype(jnp.float32)
            )


def run(kernel, name, vmem_bytes, out_shape, scratch=(), flops=10**9, **specs):
    return pl.pallas_call(
        kernel,
        out_shape=out_shape,
        scratch_shapes=scratch,
        name=name,
        **specs,
        cost_estimate=pl.CostEstimate(flops=flops, bytes_accessed=0, transcendentals=0),
        compiler_params=pltpu.CompilerParams(vmem_limit_bytes=vmem_bytes),
    )


def per_device(inputs, filter_taps, out_grad, skip_gain):
    length, chan_width = inputs.shape
    size = lax.axis_size("ctx")
    columns = lax.axis_size("chan")
    part = chan_width // size
    width = -(-part // 128) * 128
    position = lax.axis_index("ctx")
    both, back_high, back_low = tables(length)
    f32, bf16 = jnp.float32, jnp.bfloat16
    chips = sorted(range(size // 2), key=lambda chip: (-chip.bit_length(), -chip))
    order = [k for chip in chips for k in (2 * chip, 2 * chip + 1)]
    far = size // 4
    vmem_bytes = (8 + size) * 2**20

    def columns_for(array, k):
        block = lax.dynamic_slice_in_dim(array, (position ^ k) * part, part, 1)
        return jnp.pad(block, ((0, 0), (0, width - part)))

    def send(block, k):
        return lax.ppermute(block, "ctx", [(i, i ^ k) for i in range(size)])

    three = (out_grad, inputs, filter_taps)
    direct = size // 8
    rest_rows = (3 * len(chips) - 2 * direct) * length
    half = size // 2
    if width == part:
        *blocks, mine, others = run(
            functools.partial(columns_kernel, chips, direct, length, part),
            "columns", vmem_bytes,
            [jax.ShapeDtypeStruct((2 * length, width), bf16)] * (2 * direct)
            + [jax.ShapeDtypeStruct((rest_rows, width), bf16)] * 2,
        )(*[
            lax.dynamic_slice_in_dim(array, (position // half * half ^ other) * part, half * part, 1)
            for array in three
            for other in (0, half)
        ])
    else:
        blocks = [jnp.concatenate([columns_for(a, k) for a in three[:2]]) for k in order[: 2 * direct]]
        mine, others = (
            jnp.concatenate(
                [
                    columns_for(a, 2 * chip + core)
                    for i, chip in enumerate(chips)
                    for a in (three[2:] if i < direct else three)
                ]
            )
            for core in range(2)
        )

    sibling = send(others, 1)
    arrived = [send(block, k) for k, block in zip(order, blocks)]
    first_places = [(i, 0) for i in range(2 * direct)]
    taps_rows = [i * length for i in range(direct)]
    row = direct * length
    near_places = []
    for i, chip in enumerate(chips[direct:-1]):
        here = len(arrived)
        rows = (2 if i < far - direct else 3) * length
        pair = jnp.concatenate([held[row : row + rows] for held in (mine, sibling)])
        first_places += [(here, 0), (here, rows)]
        arrived.append(send(pair, 2 * chip))
        if i < far - direct:
            taps_rows.append(row + 2 * length)
        else:
            near_places += [(here, 2 * length), (here, 5 * length)]
        row += 3 * length
    first_places += [(len(arrived), row), (len(arrived) + 1, row)]
    first_arrived = [*arrived, mine, sibling]
    later = lax.optimization_barrier((mine, sibling, *arrived[: 2 * direct]))[:2]
    *tap_messages, both, back_high, back_low = run(
        functools.partial(taps_kernel, taps_rows, length),
        "taps", vmem_bytes,
        [jax.ShapeDtypeStruct((2 * length, width), bf16)] * len(taps_rows)
        + [jax.ShapeDtypeStruct(t.shape, t.dtype) for t in (both, back_high, back_low)],
    )(*later, both, back_high, back_low)
    arrived_taps = [send(block, 2 * chip) for chip, block in zip(chips, tap_messages)]
    second_places = [(i, half) for i in range(far) for half in (0, length)]
    second_places += [(ref - 2 * direct - (far - direct) + far, at) for ref, at in near_places]
    second_arrived = [*arrived_taps, *arrived[direct + far :], mine, sibling]
    second_places += [(len(second_arrived) - 2 + i, row + 2 * length) for i in range(2)]

    filter_blocks, skip, pair_spec, squares = run(
        functools.partial(first_kernel, order, length, first_places),
        "filter_gradient", vmem_bytes,
        [
            jax.ShapeDtypeStruct((size, length, width), f32),
            jax.ShapeDtypeStruct((1, width), f32),
            jax.ShapeDtypeStruct((size, 2 * length, width), f32),
            jax.ShapeDtypeStruct((8, width), f32),
        ],
        [
            pltpu.VMEM((size, 2 * length, 2 * width), f32),
            pltpu.VMEM((size, 2 * length, width), f32),
        ],
        flops=first_flops,
    )(*first_arrived, both, back_high, back_low)
    all_squares = [
        squares if k == 0 else lax.ppermute(squares, "chan", [(i, i ^ k) for i in range(columns)])
        for k in range(columns)
    ]
    coded = [
        jax.ShapeDtypeStruct((size, length, width), bf16),
        jax.ShapeDtypeStruct((size, tail_rows, width), f32),
    ]
    filter_coded = run(
        functools.partial(code_kernel, size, width), "filter_codes", vmem_bytes, coded, flops=first_flops
    )(filter_blocks, skip)
    pair_spec, *filter_coded = lax.optimization_barrier((pair_spec, *filter_coded))
    input_coded = run(
        functools.partial(second_kernel, order, length, second_places),
        "input_gradient", vmem_bytes,
        coded,
        [
            pltpu.VMEM((size, 2 * length, width), f32),
            pltpu.VMEM((size, 2 * length, width), f32),
        ],
        flops=second_flops,
    )(*second_arrived, both, back_high, back_low, pair_spec)
    messages = run(
        functools.partial(message_kernel, size, length, columns),
        "messages", vmem_bytes,
        [jax.ShapeDtypeStruct((2 * length + tail_rows, width), bf16)] * size,
    )(*filter_coded, *input_coded, *all_squares[::-1])
    messages = {k: send(message, k) if k else message for k, message in zip(order, messages)}
    nearer = sorted(chips[:far])
    turns = nearer[: far // 2] + chips[far:-1] + nearer[far // 2 :] + [0]
    turns = [k for chip in turns for k in (2 * chip, 2 * chip + 1)]

    clip_limit = 0.25 * math.sqrt(length * size * chan_width * columns)
    whole = size * width
    grad_rows, gain = out_grad, skip_gain[None, :]
    if width != part:
        spread = lambda a: jnp.pad(
            a.reshape(a.shape[0], size, part), ((0, 0), (0, 0), (0, width - part))
        ).reshape(a.shape[0], whole)
        grad_rows, gain = spread(grad_rows), spread(gain)
    turns = turns[: size // 2] + [0] + [k for k in turns[size // 2 :] if k]
    early = size // 2 + 1
    decoded = run(
        functools.partial(early_kernel, turns[:early], length, width),
        "early", vmem_bytes,
        [jax.ShapeDtypeStruct((early, length, width), f32)] * 2,
        flops=first_flops,
    )(*[messages[k] for k in turns[:early]], grad_rows, gain)
    input_grad, filter_grad, skip_grad = run(
        functools.partial(last_kernel, turns, early, length, width, clip_limit),
        "outputs", vmem_bytes,
        [
            jax.ShapeDtypeStruct((length, whole), f32),
            jax.ShapeDtypeStruct((length, whole), f32),
            jax.ShapeDtypeStruct((1, whole), f32),
        ],
    )(*[messages[k] for k in turns], *decoded, grad_rows, gain)
    if width != part:
        gather = lambda a: a.reshape(a.shape[0], size, width)[:, :, :part].reshape(
            a.shape[0], chan_width
        )
        input_grad, filter_grad, skip_grad = gather(input_grad), gather(filter_grad), gather(skip_grad)
    return (input_grad, filter_grad, skip_grad[0])


def solution(mesh):
    return jax.shard_map(
        per_device,
        mesh=mesh,
        in_specs=(P("ctx", "chan"), P("ctx", "chan"), P("ctx", "chan"), P("chan")),
        out_specs=(P("ctx", "chan"), P("ctx", "chan"), P("chan")),
        check_vma=False,
    )
```

```python
import functools
import math

import jax
import jax.numpy as jnp
import numpy as np
from jax import lax
from jax.experimental import pallas as pl
from jax.experimental.pallas import tpu as pltpu
from jax.sharding import PartitionSpec as P

epsilon = 1e-06
octaves = 246
low_power = 120
top_code = 128 * octaves - 1
tail_rows = 16
first_flops = 4 * 10**9
second_flops = 2 * 10**10


def tables(length):
    odd = 2 * np.arange(length) + 1
    phase = odd[:, None] * np.arange(length)[None, :] % (4 * length)
    angles = np.pi * phase / (2 * length)
    forward = np.concatenate([np.cos(angles), -np.sin(angles)], axis=0)
    high = forward.astype(np.float32).astype(jnp.bfloat16)
    low = (forward - high.astype(np.float64)).astype(np.float32).astype(jnp.bfloat16)
    both = np.concatenate([high, low], axis=1)
    scale = np.float32(1.0 / length)
    back_high = (high.astype(np.float32).T * scale).astype(jnp.bfloat16)
    back_low = (low.astype(np.float32).T * scale).astype(jnp.bfloat16)
    return jnp.asarray(both), jnp.asarray(back_high), jnp.asarray(back_low)


def three_parts(value):
    high = value.astype(jnp.bfloat16).astype(jnp.float32)
    rest = value - high
    middle = rest.astype(jnp.bfloat16).astype(jnp.float32)
    return high, middle, rest - middle


def encode(values):
    peak = jnp.max(jnp.abs(values), axis=0, keepdims=True) * (1.0 + 2.0**-7)
    scale = jnp.maximum(peak.astype(jnp.bfloat16).astype(jnp.float32), 2.0**-116)
    size = jnp.abs(values) * (top_code / 128.0 / scale)
    octave = jnp.floor(size)
    carrier = (size - octave + 1.0) * jnp.exp2(octave - float(low_power))
    return jnp.where(values < 0, -carrier, carrier).astype(jnp.bfloat16), scale


def decode(codes, scale):
    carrier = codes.astype(jnp.float32)
    size = jnp.abs(carrier)
    power = jnp.floor(jnp.log2(size) + 0.001)
    octaves_up = size * jnp.exp2(-power) + (power + float(low_power - 1))
    scale *= 128.0 / top_code
    return octaves_up * jnp.where(carrier < 0, -scale, scale)


def tail_tile(first_row, rows, width):
    row_ids = lax.broadcasted_iota(jnp.int32, (tail_rows, width), 0)
    tile = jnp.zeros((tail_rows, width), jnp.float32)
    for i, row in enumerate(rows):
        tile = jnp.where(
            row_ids == first_row + i, jnp.broadcast_to(row, (tail_rows, width)), tile
        )
    return tile


def correlate_rows(pairs, others, size):
    sums = [real + imag for real, imag in pairs]
    turned = [(real, real - imag, real + imag) for real, imag in others]
    results = []
    for p in range(size):
        shared = first = second = None
        for q in range(p, size):
            real, less, more = turned[q - p]
            terms = sums[q] * real, pairs[q][1] * less, pairs[q][0] * more
            if q > p:
                terms = shared + terms[0], first + terms[1], second + terms[2]
            shared, first, second = terms
        results.append((shared - first, shared - second))
    return results


def send_results(position, order, acc, back_high, back_low, emit):
    width = acc.shape[2]
    for i in range(0, len(order), 2):
        spec = jnp.concatenate([acc[position ^ order[i]], acc[position ^ order[i + 1]]], axis=1)
        high = spec.astype(jnp.bfloat16)
        low = (spec - high.astype(jnp.float32)).astype(jnp.bfloat16)
        dot = functools.partial(jnp.dot, preferred_element_type=jnp.float32)
        block = dot(back_high[...], high) + dot(back_high[...], low) + dot(back_low[...], high)
        emit(i, block[:, :width])
        emit(i + 1, block[:, width:])


def columns_kernel(chips, direct, length, part, *refs):
    halves, blocks, rest = refs[:6], refs[6:-2], refs[-2:]
    position = lax.axis_index("ctx")
    half = len(chips)

    def put(out, row, j, k):
        columns = pl.ds(pl.multiple_of((position ^ k) % half * part, part), part)
        out[row : row + length] = halves[2 * j + k // half][:, columns]

    for core in range(2):
        row = 0
        for i, chip in enumerate(chips):
            for j in range(3):
                if i < direct and j < 2:
                    put(blocks[2 * i + core], j * length, j, 2 * chip + core)
                else:
                    put(rest[core], row, j, 2 * chip + core)
                    row += length


def taps_kernel(rows, length, mine, sibling, *refs):
    tables, messages, held = refs[:3], refs[3:-3], refs[-3:]
    for table, place in zip(tables, held):
        place[...] = table[...]
    for row, message in zip(rows, messages):
        message[:length] = mine[row : row + length]
        message[length:] = sibling[row : row + length]


def first_kernel(order, length, places, *refs):
    size = len(order)
    both, back_high, back_low, blocks_out, skip_out, pair_spec, squares, spec, acc = refs[-9:]
    width = spec.shape[2] // 2
    position = lax.axis_index("ctx")

    skip = jnp.zeros((1, width), jnp.float32)
    for i, k in enumerate(order):
        ref, row = places[i]
        grad, other = refs[ref][row : row + length], refs[ref][row + length : row + 2 * length]
        skip += jnp.sum(grad.astype(jnp.float32) * other.astype(jnp.float32), axis=0, keepdims=True)
        lanes = jnp.concatenate([grad, other], axis=1)
        spec[position ^ k] = jnp.dot(
            both[...], jnp.concatenate([lanes, lanes], axis=0), preferred_element_type=jnp.float32
        )

    flip = jnp.where(lax.broadcasted_iota(jnp.int32, (8, width), 0) % 2 == 0, 1.0, -1.0)

    def rows(r, carry):
        real_rows = pl.ds(pl.multiple_of(r * 8, 8), 8)
        imag_rows = pl.ds(pl.multiple_of(length + r * 8, 8), 8)
        grad = [(spec[q, real_rows, :width], spec[q, imag_rows, :width]) for q in range(size)]
        pairs = []
        for q in range(size):
            if q + 1 < size:
                real = grad[q][0] + flip * grad[q + 1][1]
                imag = grad[q][1] - flip * grad[q + 1][0]
            else:
                real, imag = grad[q]
            pair_spec[q, real_rows, :] = real
            pair_spec[q, imag_rows, :] = imag
            pairs.append((real, imag))
        others = [(spec[q, real_rows, width:], spec[q, imag_rows, width:]) for q in range(size)]
        for p, (real, imag) in enumerate(correlate_rows(pairs, others, size)):
            acc[p, real_rows, :] = real
            acc[p, imag_rows, :] = imag
        return carry

    lax.fori_loop(0, length // 8, rows, 0, unroll=2)
    skip_out[...] = skip
    squares[...] = jnp.zeros_like(squares)

    def emit(i, block):
        squares[...] += jnp.sum((block * block).reshape(length // 8, 8, width), axis=0)
        blocks_out[i] = block

    send_results(position, order, acc, back_high, back_low, emit)


def code_kernel(size, width, blocks, skip, filter_codes, filter_tails):
    skip_parts = three_parts(skip[...])
    for i in range(size):
        filter_codes[i], scale = encode(blocks[i])
        filter_tails[i] = tail_tile(0, (scale,) + skip_parts, width)


def second_kernel(order, length, places, *refs):
    size = len(order)
    both, back_high, back_low, pair_spec, input_codes, input_tails, spec, acc = refs[-8:]
    width = spec.shape[2]
    position = lax.axis_index("ctx")

    for i in range(0, size, 2):
        lanes = jnp.concatenate(
            [refs[ref][row : row + length] for ref, row in places[i : i + 2]], axis=1
        )
        both_specs = jnp.dot(
            both[...], jnp.concatenate([lanes, lanes], axis=0), preferred_element_type=jnp.float32
        )
        spec[position ^ order[i]] = both_specs[:, :width]
        spec[position ^ order[i + 1]] = both_specs[:, width:]

    def rows(r, carry):
        real_rows = pl.ds(pl.multiple_of(r * 8, 8), 8)
        imag_rows = pl.ds(pl.multiple_of(length + r * 8, 8), 8)
        pairs = [(pair_spec[q, real_rows, :], pair_spec[q, imag_rows, :]) for q in range(size)]
        others = [(spec[q, real_rows, :], spec[q, imag_rows, :]) for q in range(size)]
        for p, (real, imag) in enumerate(correlate_rows(pairs, others, size)):
            acc[p, real_rows, :] = real
            acc[p, imag_rows, :] = imag
        return carry

    lax.fori_loop(0, length // 8, rows, 0, unroll=2)

    def emit(i, block):
        input_codes[i], scale = encode(block)
        input_tails[i] = tail_tile(4, (scale,), width)

    send_results(position, order, acc, back_high, back_low, emit)


def message_kernel(size, length, sums, *refs):
    filter_codes, filter_tails, input_codes, input_tails = refs[:4]
    partial_squares, out = refs[4 : 4 + sums], refs[4 + sums :]
    squares = partial_squares[0][...]
    for other in partial_squares[1:]:
        squares += other[...]
    total = jnp.sum(jnp.sum(squares, axis=0, keepdims=True), axis=1, keepdims=True)
    total = jnp.minimum(total, 3.38e38)
    width = squares.shape[1]
    total_rows = tail_tile(5, three_parts(jnp.broadcast_to(total, (1, width))), width)
    for i in range(size):
        out[i][:length] = filter_codes[i]
        out[i][length : 2 * length] = input_codes[i]
        tail = filter_tails[i] + input_tails[i] + total_rows
        out[i][2 * length :] = tail.astype(jnp.bfloat16)


def early_kernel(order, length, part, *refs):
    messages, (grad, gain, input_blocks, filter_blocks) = refs[:-4], refs[-4:]
    position = lax.axis_index("ctx")
    for i, (k, message) in enumerate(zip(order, messages)):
        columns = pl.ds(pl.multiple_of((position ^ k) * part, part), part)
        tail = message[2 * length :].astype(jnp.float32)
        filter_blocks[i] = decode(message[:length], tail[0:1])
        input_blocks[i] = (
            decode(message[length : 2 * length], tail[4:5])
            + gain[:, columns] * grad[:, columns].astype(jnp.float32)
        )


def last_kernel(order, early, length, part, clip_limit, *refs):
    size = len(order)
    messages = refs[:size]
    input_blocks, filter_blocks, grad, gain, input_grad, filter_grad, skip_grad = refs[size:]
    position = lax.axis_index("ctx")
    total = jnp.zeros((1, part), jnp.float32)
    for message in messages:
        tail = message[2 * length :].astype(jnp.float32)
        total += tail[5:6] + tail[6:7] + tail[7:8]
    factor = jnp.minimum(1.0, clip_limit / jnp.sqrt(total + epsilon))
    for i, (k, message) in enumerate(zip(order, messages)):
        columns = pl.ds(pl.multiple_of((position ^ k) * part, part), part)
        tail = message[2 * length :].astype(jnp.float32)
        skip_grad[:, columns] = tail[1:2] + tail[2:3] + tail[3:4]
        if i < early:
            filter_grad[:, columns] = filter_blocks[i] * factor
            input_grad[:, columns] = input_blocks[i]
        else:
            filter_grad[:, columns] = decode(message[:length], tail[0:1]) * factor
            input_grad[:, columns] = (
                decode(message[length : 2 * length], tail[4:5])
                + gain[:, columns] * grad[:, columns].astype(jnp.float32)
            )


def run(kernel, name, vmem_bytes, out_shape, scratch=(), flops=10**9, **specs):
    return pl.pallas_call(
        kernel,
        out_shape=out_shape,
        scratch_shapes=scratch,
        name=name,
        **specs,
        cost_estimate=pl.CostEstimate(flops=flops, bytes_accessed=0, transcendentals=0),
        compiler_params=pltpu.CompilerParams(vmem_limit_bytes=vmem_bytes),
    )


def per_device(inputs, filter_taps, out_grad, skip_gain):
    length, chan_width = inputs.shape
    size = lax.axis_size("ctx")
    columns = lax.axis_size("chan")
    part = chan_width // size
    width = -(-part // 128) * 128
    position = lax.axis_index("ctx")
    both, back_high, back_low = tables(length)
    f32, bf16 = jnp.float32, jnp.bfloat16
    chips = sorted(range(size // 2), key=lambda chip: (-chip.bit_length(), -chip))
    order = [k for chip in chips for k in (2 * chip, 2 * chip + 1)]
    far = size // 4
    vmem_bytes = (8 + size) * 2**20

    def columns_for(array, k):
        block = lax.dynamic_slice_in_dim(array, (position ^ k) * part, part, 1)
        return jnp.pad(block, ((0, 0), (0, width - part)))

    def send(block, k):
        return lax.ppermute(block, "ctx", [(i, i ^ k) for i in range(size)])

    three = (out_grad, inputs, filter_taps)
    direct = size // 8
    rest_rows = (3 * len(chips) - 2 * direct) * length
    half = size // 2
    if width == part:
        *blocks, mine, others = run(
            functools.partial(columns_kernel, chips, direct, length, part),
            "columns", vmem_bytes,
            [jax.ShapeDtypeStruct((2 * length, width), bf16)] * (2 * direct)
            + [jax.ShapeDtypeStruct((rest_rows, width), bf16)] * 2,
        )(*[
            lax.dynamic_slice_in_dim(array, (position // half * half ^ other) * part, half * part, 1)
            for array in three
            for other in (0, half)
        ])
    else:
        blocks = [jnp.concatenate([columns_for(a, k) for a in three[:2]]) for k in order[: 2 * direct]]
        mine, others = (
            jnp.concatenate(
                [
                    columns_for(a, 2 * chip + core)
                    for i, chip in enumerate(chips)
                    for a in (three[2:] if i < direct else three)
                ]
            )
            for core in range(2)
        )

    sibling = send(others, 1)
    arrived = [send(block, k) for k, block in zip(order, blocks)]
    first_places = [(i, 0) for i in range(2 * direct)]
    taps_rows = [i * length for i in range(direct)]
    row = direct * length
    near_places = []
    for i, chip in enumerate(chips[direct:-1]):
        here = len(arrived)
        rows = (2 if i < far - direct else 3) * length
        pair = jnp.concatenate([held[row : row + rows] for held in (mine, sibling)])
        first_places += [(here, 0), (here, rows)]
        arrived.append(send(pair, 2 * chip))
        if i < far - direct:
            taps_rows.append(row + 2 * length)
        else:
            near_places += [(here, 2 * length), (here, 5 * length)]
        row += 3 * length
    first_places += [(len(arrived), row), (len(arrived) + 1, row)]
    first_arrived = [*arrived, mine, sibling]
    later = lax.optimization_barrier((mine, sibling, *arrived[: 2 * direct]))[:2]
    *tap_messages, both, back_high, back_low = run(
        functools.partial(taps_kernel, taps_rows, length),
        "taps", vmem_bytes,
        [jax.ShapeDtypeStruct((2 * length, width), bf16)] * len(taps_rows)
        + [jax.ShapeDtypeStruct(t.shape, t.dtype) for t in (both, back_high, back_low)],
    )(*later, both, back_high, back_low)
    arrived_taps = [send(block, 2 * chip) for chip, block in zip(chips, tap_messages)]
    second_places = [(i, half) for i in range(far) for half in (0, length)]
    second_places += [(ref - 2 * direct - (far - direct) + far, at) for ref, at in near_places]
    second_arrived = [*arrived_taps, *arrived[direct + far :], mine, sibling]
    second_places += [(len(second_arrived) - 2 + i, row + 2 * length) for i in range(2)]

    filter_blocks, skip, pair_spec, squares = run(
        functools.partial(first_kernel, order, length, first_places),
        "filter_gradient", vmem_bytes,
        [
            jax.ShapeDtypeStruct((size, length, width), f32),
            jax.ShapeDtypeStruct((1, width), f32),
            jax.ShapeDtypeStruct((size, 2 * length, width), f32),
            jax.ShapeDtypeStruct((8, width), f32),
        ],
        [
            pltpu.VMEM((size, 2 * length, 2 * width), f32),
            pltpu.VMEM((size, 2 * length, width), f32),
        ],
        flops=first_flops,
    )(*first_arrived, both, back_high, back_low)
    all_squares = [
        squares if k == 0 else lax.ppermute(squares, "chan", [(i, i ^ k) for i in range(columns)])
        for k in range(columns)
    ]
    coded = [
        jax.ShapeDtypeStruct((size, length, width), bf16),
        jax.ShapeDtypeStruct((size, tail_rows, width), f32),
    ]
    filter_coded = run(
        functools.partial(code_kernel, size, width), "filter_codes", vmem_bytes, coded, flops=first_flops
    )(filter_blocks, skip)
    pair_spec, *filter_coded = lax.optimization_barrier((pair_spec, *filter_coded))
    input_coded = run(
        functools.partial(second_kernel, order, length, second_places),
        "input_gradient", vmem_bytes,
        coded,
        [
            pltpu.VMEM((size, 2 * length, width), f32),
            pltpu.VMEM((size, 2 * length, width), f32),
        ],
        flops=second_flops,
    )(*second_arrived, both, back_high, back_low, pair_spec)
    messages = run(
        functools.partial(message_kernel, size, length, columns),
        "messages", vmem_bytes,
        [jax.ShapeDtypeStruct((2 * length + tail_rows, width), bf16)] * size,
    )(*filter_coded, *input_coded, *all_squares[::-1])
    messages = {k: send(message, k) if k else message for k, message in zip(order, messages)}
    nearer = sorted(chips[:far])
    turns = nearer[: far // 2] + chips[far:-1] + nearer[far // 2 :] + [0]
    turns = [k for chip in turns for k in (2 * chip, 2 * chip + 1)]

    clip_limit = 0.25 * math.sqrt(length * size * chan_width * columns)
    whole = size * width
    grad_rows, gain = out_grad, skip_gain[None, :]
    if width != part:
        spread = lambda a: jnp.pad(
            a.reshape(a.shape[0], size, part), ((0, 0), (0, 0), (0, width - part))
        ).reshape(a.shape[0], whole)
        grad_rows, gain = spread(grad_rows), spread(gain)
    early = size // 2 + 2
    turns = turns[: early - 1] + [0] + [k for k in turns[early - 1 :] if k]
    decoded = run(
        functools.partial(early_kernel, turns[:early], length, width),
        "early", vmem_bytes,
        [jax.ShapeDtypeStruct((early, length, width), f32)] * 2,
        flops=first_flops,
    )(*[messages[k] for k in turns[:early]], grad_rows, gain)
    input_grad, filter_grad, skip_grad = run(
        functools.partial(last_kernel, turns, early, length, width, clip_limit),
        "outputs", vmem_bytes,
        [
            jax.ShapeDtypeStruct((length, whole), f32),
            jax.ShapeDtypeStruct((length, whole), f32),
            jax.ShapeDtypeStruct((1, whole), f32),
        ],
    )(*[messages[k] for k in turns], *decoded, grad_rows, gain)
    if width != part:
        gather = lambda a: a.reshape(a.shape[0], size, width)[:, :, :part].reshape(
            a.shape[0], chan_width
        )
        input_grad, filter_grad, skip_grad = gather(input_grad), gather(filter_grad), gather(skip_grad)
    return (input_grad, filter_grad, skip_grad[0])


def solution(mesh):
    return jax.shard_map(
        per_device,
        mesh=mesh,
        in_specs=(P("ctx", "chan"), P("ctx", "chan"), P("ctx", "chan"), P("chan")),
        out_specs=(P("ctx", "chan"), P("ctx", "chan"), P("chan")),
        check_vma=False,
    )
```
